32 devices in a mesh: req: 2 (over y), ctx: 16 (over z, x, core).
Axes of the slice: x: 2, y: 2, z: 4, core: 2. Of those that a mesh axis runs over, the one named last changes fastest.
Arguments:
- q_latent: bfloat16 [128, 48, 512], P(None, 'req'), parts along dimension 1, may hold values from -64 to 64
- q_rope: bfloat16 [128, 3072], P(None, 'req'), parts along dimension 1, may hold values from -6 to 6
- cache_latent: bfloat16 [128, 128, 512], P(('req', 'ctx')), parts along dimension 0, may hold values from -6 to 6
- cache_rope: bfloat16 [128, 64, 128], P(('req', 'ctx')), parts along dimension 0, may hold values from -6 to 6
- new_latent: bfloat16 [48, 512], P('req'), parts along dimension 0, may hold values from -6 to 6
- new_rope: bfloat16 [48, 64], P('req'), parts along dimension 0, may hold values from -6 to 6
- removed: int32 [24, 2], P('req'), parts along dimension 0, may hold values from 1 to 63, as said below
Outputs:
- attended: bfloat16 [128, 48, 512], P('ctx', 'req'), parts along dimension 1
The draws below stay inside these ranges and needn't reach their ends.
There are 2 independent parts, one for each index of `req`. The reference program is written for one: setup_inputs(seed, part) draws one part's arguments, and reference() takes and returns one part's arrays. A program takes and returns all parts, laid end to end along the dimension named above; each array names one. Nothing has to cross between parts.
Inputs may be any that keep to these rules, and one draw needn't show every extreme that they name: Each row (first, last) names the blocks first to last - 1 of one removed span of whole blocks. Rows ascend, the spans are disjoint and are parted by at least one kept block; the first span starts at block 1 and the last ends at block 63.
All inputs are finite; a program needn't handle non-finite values.
Results may differ from the reference program's by a relative error of at most 0.0024.
Values may be sent and summed in bfloat16 or wider, within the bound.
A program may use at most 64 MiB of HBM per device.

```python
import jax
import jax.numpy as jnp
import numpy as np
from jax import lax

H = 128
LAT = 512
ROPE = 64
BLK = 128
NEW = 24
SPANS = 12
NBLK = 64
CTX = 8192


def shared_values(key):
    cache_seed = jax.random.fold_in(key, 11)
    fresh_seed = jax.random.fold_in(key, 12)
    query_seed = jax.random.fold_in(key, 13)
    strength_seed = jax.random.fold_in(key, 14)
    cache_values = jnp.clip(jax.random.normal(cache_seed, (NBLK, BLK, LAT), jnp.float32), -6.0, 6.0)
    cache_values = cache_values.astype(jnp.bfloat16).astype(jnp.float32)
    fresh_values = jnp.clip(jax.random.normal(fresh_seed, (NEW, LAT), jnp.float32), -6.0, 6.0)
    fresh_values = fresh_values.astype(jnp.bfloat16).astype(jnp.float32)
    widening = 512.0 / LAT
    strength = jnp.exp(jax.random.uniform(strength_seed, (H,), jnp.float32, jnp.log(0.1), jnp.log(0.4)))
    noise_part = jnp.clip(jax.random.normal(query_seed, (H, NEW, LAT), jnp.float32), -6.0, 6.0) * 1.5 * jnp.sqrt(widening)
    queries = noise_part + strength[:, None, None] * fresh_values[None, :, :]
    return (cache_values, fresh_values, queries)


def draw_q_latent(key, part):
    cache_values, fresh_values, queries = shared_values(key)
    return jnp.clip(queries, -64.0, 64.0).astype(jnp.bfloat16)


def draw_cache_latent(key, part):
    return shared_values(key)[0].astype(jnp.bfloat16)


def draw_new_latent(key, part):
    return shared_values(key)[1].astype(jnp.bfloat16)


def draw_removed(key, part):
    interior = jax.random.permutation(jax.random.fold_in(key, 21), NBLK - 3)[:2 * SPANS - 2] + 2
    bounds = jnp.sort(jnp.concatenate([jnp.array([1, NBLK - 1], jnp.int32), interior.astype(jnp.int32)]))
    return bounds.reshape(SPANS, 2)


def block_levels(key, shape, pieces, least, top_value):
    def one(position, parts):
        heights = jax.random.uniform(jax.random.fold_in(jax.random.fold_in(key, 6), position), (parts,), jnp.float32, least / len(pieces), top_value / len(pieces))
        return jnp.repeat(jnp.exp(heights), shape[position] // parts).reshape((-1,) + (1,) * (len(shape) - position - 1))

    factor_of = one(*pieces[0])
    for cut in pieces[1:]:
        factor_of = factor_of * one(*cut)
    return factor_of


def noise(rng, dims, scale, limit, pieces=(), held_as=jnp.bfloat16):
    values = scale * jax.random.normal(rng, dims, jnp.float32)
    if pieces:
        values = values * block_levels(rng, dims, pieces, -0.22, 0.18)
    return jnp.clip(values, -limit, limit).astype(held_as)


def setup_inputs(seed: int = 0, part: int = 0) -> dict:
    key_of = jax.random.split(jax.random.key(seed), 8)
    own_keys = jax.random.split(jax.random.fold_in(key_of[7], part), 8)
    q_latent = draw_q_latent(jax.random.fold_in(jax.random.fold_in(key_of[7], part), 71), part)
    q_rope = noise(own_keys[1], (H, NEW * ROPE), 1.0, 6.0)
    cache_latent = draw_cache_latent(jax.random.fold_in(jax.random.fold_in(key_of[7], part), 71), part)
    cache_rope = noise(own_keys[3], (NBLK, ROPE, BLK), 1.0, 6.0, ((0, 16),))
    new_latent = draw_new_latent(jax.random.fold_in(jax.random.fold_in(key_of[7], part), 71), part)
    new_rope = noise(own_keys[5], (NEW, ROPE), 1.0, 6.0)
    removed = draw_removed(jax.random.fold_in(jax.random.fold_in(key_of[7], part), 71), part)
    return dict(q_latent=q_latent, q_rope=q_rope, cache_latent=cache_latent, cache_rope=cache_rope, new_latent=new_latent, new_rope=new_rope, removed=removed)


floor_value = -1.0e30
score_scale = 192.0 ** -0.5


def rope_tables(rope_width):
    halves = rope_width // 2
    frequencies = 10000.0 ** (-2.0 * np.arange(halves) / rope_width)
    coarse = np.mod(4096.0 * frequencies, 2.0 * np.pi)
    middle = np.mod(64.0 * frequencies, 2.0 * np.pi)
    return jnp.asarray(frequencies, jnp.float32), jnp.asarray(coarse, jnp.float32), jnp.asarray(middle, jnp.float32)


def turn_angles(shift_rows, rope_width):
    frequencies, coarse, middle = rope_tables(rope_width)
    magnitude = jnp.abs(shift_rows)
    signed = jnp.where(shift_rows < 0, -1.0, 1.0).astype(jnp.float32)
    upper_part = (magnitude // 4096).astype(jnp.float32)[..., None]
    centre_part = ((magnitude // 64) % 64).astype(jnp.float32)[..., None]
    lowest_part = (magnitude % 64).astype(jnp.float32)[..., None]
    angles = upper_part * coarse + centre_part * middle + lowest_part * frequencies
    return jnp.cos(angles), signed[..., None] * jnp.sin(angles)


def rotate_last(values, cosine, sine_part):
    halves = values.shape[-1] // 2
    first_half = values[..., :halves]
    second_half = values[..., halves:]
    return jnp.concatenate([first_half * cosine - second_half * sine_part, first_half * sine_part + second_half * cosine], axis=-1)


def rotate_middle(values, cosine, sine_part):
    halves = values.shape[1] // 2
    first_half = values[:, :halves, :]
    second_half = values[:, halves:, :]
    return jnp.concatenate([first_half * cosine - second_half * sine_part, first_half * sine_part + second_half * cosine], axis=1)


def span_info(removed, total_blocks, block_rows):
    starts = removed[:, 0]
    finishes = removed[:, 1]
    block_ids = jnp.arange(total_blocks, dtype=jnp.int32)
    inside = (block_ids[:, None] >= starts[None, :]) & (block_ids[:, None] < finishes[None, :])
    kept_block = jnp.logical_not(jnp.any(inside, axis=1))
    drop_before = block_rows * jnp.sum(jnp.clip(block_ids[:, None], starts[None, :], finishes[None, :]) - starts[None, :], axis=1)
    kept_rows = total_blocks * block_rows - block_rows * jnp.sum(finishes - starts)
    return kept_block, drop_before.astype(jnp.int32), kept_rows.astype(jnp.int32)


def reference(q_latent, q_rope, cache_latent, cache_rope, new_latent, new_rope, removed):
    kept_block, drop_before, kept_rows = span_info(removed, NBLK, BLK)
    cosine, sine_part = turn_angles(-drop_before, ROPE)
    cache_keys = rotate_middle(cache_rope.astype(jnp.float32), cosine[:, :, None], sine_part[:, :, None]).astype(jnp.bfloat16)
    positions = kept_rows + jnp.arange(NEW, dtype=jnp.int32)
    query_cos, query_sin = turn_angles(positions, ROPE)
    queries_rope = rotate_last(q_rope.reshape(H, NEW, ROPE).astype(jnp.float32), query_cos, query_sin).astype(jnp.bfloat16)
    new_keys = rotate_last(new_rope.astype(jnp.float32), query_cos, query_sin).astype(jnp.bfloat16)
    latent_cols = cache_latent.reshape(CTX, LAT).T
    key_cols = jnp.transpose(cache_keys, (1, 0, 2)).reshape(ROPE, CTX)
    latent_blocks = cache_latent.astype(jnp.float32)
    causal = jnp.arange(NEW, dtype=jnp.int32)[None, :] <= jnp.arange(NEW, dtype=jnp.int32)[:, None]
    kept_flags = kept_block[None, :]

    def one_head(operands):
        head_latent, head_rope = operands
        scores = (jnp.dot(head_latent, latent_cols, preferred_element_type=jnp.float32) + jnp.dot(head_rope, key_cols, preferred_element_type=jnp.float32)) * score_scale
        scores = scores.reshape(NEW, NBLK, BLK)
        block_max = jnp.max(scores, axis=2)
        weights = jnp.exp(scores - block_max[:, :, None]).astype(jnp.bfloat16)
        block_sum = jnp.sum(weights.astype(jnp.float32), axis=2)
        block_out = jnp.einsum('tbr,brd->tbd', weights.astype(jnp.float32), latent_blocks)
        new_scores = (jnp.dot(head_latent, new_latent.T, preferred_element_type=jnp.float32) + jnp.dot(head_rope, new_keys.T, preferred_element_type=jnp.float32)) * score_scale
        masked = jnp.where(causal, new_scores, floor_value)
        new_max = jnp.max(masked, axis=1)
        new_weights = jnp.where(causal, jnp.exp(masked - new_max[:, None]), 0.0).astype(jnp.bfloat16)
        new_sum = jnp.sum(new_weights.astype(jnp.float32), axis=1)
        new_out = jnp.dot(new_weights, new_latent, preferred_element_type=jnp.float32)
        lifted = jnp.where(kept_flags, block_max, floor_value)
        top_score = jnp.maximum(jnp.max(lifted, axis=1), new_max)
        block_part = jnp.where(kept_flags, jnp.exp(lifted - top_score[:, None]), 0.0)
        new_part = jnp.exp(new_max - top_score)
        numerator = jnp.sum(block_out * block_part[:, :, None], axis=1) + new_out * new_part[:, None]
        denominator = jnp.sum(block_sum * block_part, axis=1) + new_sum * new_part
        return (numerator / denominator[:, None]).astype(jnp.bfloat16)

    return lax.map(one_head, (q_latent, queries_rope))
```

```python
import jax
import jax.numpy as jnp
import numpy as np
from jax import lax
from jax.experimental import pallas as pl
from jax.experimental.pallas import tpu as pltpu
from jax.sharding import PartitionSpec as P

floor_value = -1e30
score_scale = 192.0 ** (-0.5)


def rope_tables(rope_width):
    halves = rope_width // 2
    frequencies = 10000.0 ** (-2.0 * np.arange(halves) / rope_width)
    coarse = np.mod(4096.0 * frequencies, 2.0 * np.pi)
    middle = np.mod(64.0 * frequencies, 2.0 * np.pi)
    return (
        jnp.asarray(frequencies, jnp.float32),
        jnp.asarray(coarse, jnp.float32),
        jnp.asarray(middle, jnp.float32),
    )


def turn_angles(shift_rows, rope_width):
    frequencies, coarse, middle = rope_tables(rope_width)
    magnitude = jnp.abs(shift_rows)
    signed = jnp.where(shift_rows < 0, -1.0, 1.0).astype(jnp.float32)
    upper_part = (magnitude // 4096).astype(jnp.float32)[..., None]
    centre_part = (magnitude // 64 % 64).astype(jnp.float32)[..., None]
    lowest_part = (magnitude % 64).astype(jnp.float32)[..., None]
    angles = upper_part * coarse + centre_part * middle + lowest_part * frequencies
    return (jnp.cos(angles), signed[..., None] * jnp.sin(angles))


def rotate_last(values, cosine, sine_part):
    halves = values.shape[-1] // 2
    first_half = values[..., :halves]
    second_half = values[..., halves:]
    return jnp.concatenate(
        [
            first_half * cosine - second_half * sine_part,
            first_half * sine_part + second_half * cosine,
        ],
        axis=-1,
    )


def rotate_middle(values, cosine, sine_part):
    halves = values.shape[1] // 2
    first_half = values[:, :halves, :]
    second_half = values[:, halves:, :]
    return jnp.concatenate(
        [
            first_half * cosine - second_half * sine_part,
            first_half * sine_part + second_half * cosine,
        ],
        axis=1,
    )


def span_info(removed, total_blocks, block_rows):
    starts = removed[:, 0]
    finishes = removed[:, 1]
    block_ids = jnp.arange(total_blocks, dtype=jnp.int32)
    inside = (block_ids[:, None] >= starts[None, :]) & (block_ids[:, None] < finishes[None, :])
    kept_block = jnp.logical_not(jnp.any(inside, axis=1))
    drop_before = block_rows * jnp.sum(
        jnp.clip(block_ids[:, None], starts[None, :], finishes[None, :]) - starts[None, :], axis=1
    )
    kept_rows = total_blocks * block_rows - block_rows * jnp.sum(finishes - starts)
    return (kept_block, drop_before, kept_rows)


code_limit = 32767.0
tiny_peak = 1e-30
nt_dims = (((1,), (1,)), ((), ()))


def local_state(q, qr, lat_ref, keys, flag_ref):
    blocks, block_rows, lat_width = lat_ref.shape
    latents = lat_ref[...].reshape(blocks * block_rows, lat_width)
    scores = (
        lax.dot_general(q, latents, nt_dims, preferred_element_type=jnp.float32)
        + jnp.dot(qr, keys, preferred_element_type=jnp.float32)
    ) * score_scale
    lifted, sums, outs = [], [], []
    for b in range(blocks):
        part = scores[:, b * block_rows : (b + 1) * block_rows]
        block_max = jnp.max(part, axis=1, keepdims=True)
        weights = jnp.exp(part - block_max).astype(jnp.bfloat16)
        sums.append(jnp.sum(weights.astype(jnp.float32), axis=1, keepdims=True))
        outs.append(jnp.dot(weights, lat_ref[b], preferred_element_type=jnp.float32))
        lifted.append(jnp.where(flag_ref[b] > 0, block_max, floor_value))
    top = lifted[0]
    for b in range(1, blocks):
        top = jnp.maximum(top, lifted[b])
    total, acc = 0.0, 0.0
    for b in range(blocks):
        factor = jnp.where(flag_ref[b] > 0, jnp.exp(lifted[b] - top), 0.0)
        total = total + sums[b] * factor
        acc = acc + outs[b] * factor
    return top, total, acc


def merge(one, other):
    top = jnp.maximum(one[0], other[0])
    left, right = jnp.exp(one[0] - top), jnp.exp(other[0] - top)
    return top, one[1] * left + other[1] * right, one[2] * left + other[2] * right


def put_state(state, code_ref, meta_ref, slot):
    top, total, acc = state
    rows = acc.shape[0]
    peak = jnp.maximum(jnp.max(jnp.abs(acc), axis=1, keepdims=True), tiny_peak)
    code_ref[slot] = jnp.round(acc * (code_limit / peak)).astype(jnp.int32).astype(jnp.int16)
    lane = lax.broadcasted_iota(jnp.int32, (rows, 128), 1)
    packed = jnp.where(lane == 0, top, jnp.where(lane == 1, total, peak * (1.0 / code_limit)))
    spare = meta_ref.shape[2] - rows
    if spare:
        packed = jnp.concatenate([packed, jnp.zeros((spare, 128), jnp.float32)], axis=0)
    meta_ref[slot] = packed.T[:8]


def get_state(code_ref, meta_ref, slot):
    rows = code_ref.shape[1]
    meta = meta_ref[slot]
    meta = jnp.concatenate([meta, jnp.zeros((120, meta.shape[1]), jnp.float32)], axis=0).T[:rows]
    acc = code_ref[slot].astype(jnp.int32).astype(jnp.float32) * meta[:, 2:3]
    return meta[:, 0:1], meta[:, 1:2], acc


def new_state(q, qr, lat, keys, tokens):
    rows = q.shape[0]
    scores = (
        lax.dot_general(q, lat, nt_dims, preferred_element_type=jnp.float32)
        + lax.dot_general(qr, keys, nt_dims, preferred_element_type=jnp.float32)
    ) * score_scale
    token = lax.broadcasted_iota(jnp.int32, (rows, tokens), 0) % tokens
    causal = lax.broadcasted_iota(jnp.int32, (rows, tokens), 1) <= token
    masked = jnp.where(causal, scores, floor_value)
    top = jnp.max(masked, axis=1, keepdims=True)
    weights = jnp.where(causal, jnp.exp(masked - top), 0.0).astype(jnp.bfloat16)
    total = jnp.sum(weights.astype(jnp.float32), axis=1, keepdims=True)
    return top, total, jnp.dot(weights, lat, preferred_element_type=jnp.float32)


def exchange_kernel(
    far, tokens, q_ref, qr_ref, lat_ref, key_ref, flag_ref, new_lat_ref, new_key_ref, out_ref,
    core_out, core_in, core_out_meta, core_in_meta,
    pair_out, pair_in, pair_out_meta, pair_in_meta,
    far_out, far_in, far_out_meta, far_in_meta,
    core_sems, pair_sems, far_sems,
):
    me = lax.axis_index("ctx")
    core, pair, place = me % 2, (me // 2) % 2, me // 4

    def index_of(place_id, pair_id, core_id):
        return (place_id * 2 + pair_id) * 2 + core_id

    def place_at(step):
        return (place + 1 + step) % far

    sibling = index_of(place, pair, 1 - core)
    partner = index_of(place, 1 - pair, core)
    barrier = pltpu.get_barrier_semaphore()
    for other in [sibling, partner]:
        pl.semaphore_signal(barrier, 1, device_id={"ctx": other})

    def greet(step, nothing):
        pl.semaphore_signal(barrier, 1, device_id={"ctx": index_of(place_at(step), pair, core)})
        return nothing

    lax.fori_loop(0, far - 1, greet, 0)
    pl.semaphore_wait(barrier, far + 1)

    def copies(source, landing, source_meta, landing_meta, sems, slot, target):
        return [
            pltpu.make_async_remote_copy(
                src_ref=a.at[slot],
                dst_ref=b.at[slot],
                send_sem=sems.at[2 * kind, slot],
                recv_sem=sems.at[2 * kind + 1, slot],
                device_id={"ctx": target},
            )
            for kind, (a, b) in enumerate([(source, landing), (source_meta, landing_meta)])
        ]

    def core_copies(slot):
        return copies(core_out, core_in, core_out_meta, core_in_meta, core_sems, slot, sibling)

    def pair_copies(slot):
        return copies(pair_out, pair_in, pair_out_meta, pair_in_meta, pair_sems, slot, partner)

    def far_copies(slot):
        target = index_of(place_at(slot), pair, core)
        return copies(far_out, far_in, far_out_meta, far_in_meta, far_sems, slot, target)

    def start(both):
        for copy in both:
            copy.start()

    def landed(both):
        for copy in both:
            copy.wait_recv()

    def own_state(owner):
        return local_state(q_ref[owner], qr_ref[owner], lat_ref, key_ref[...], flag_ref)

    def to_core(pair_id, first):
        def step_of(step, nothing):
            state = own_state(index_of(place_at(step), pair_id, 1 - core))
            put_state(state, core_out, core_out_meta, first + step)
            start(core_copies(first + step))
            return nothing

        lax.fori_loop(0, far, step_of, 0)

    to_core(1 - pair, 0)

    def to_pair(step, nothing):
        state = own_state(index_of(place_at(step), 1 - pair, core))
        landed(core_copies(step))
        state = merge(state, get_state(core_in, core_in_meta, step))
        put_state(state, pair_out, pair_out_meta, step)
        start(pair_copies(step))
        return nothing

    lax.fori_loop(0, far, to_pair, 0)
    to_core(pair, far)

    def gathered(step):
        state = own_state(index_of(place_at(step), pair, core))
        landed(core_copies(far + step))
        state = merge(state, get_state(core_in, core_in_meta, far + step))
        landed(pair_copies(step))
        return merge(state, get_state(pair_in, pair_in_meta, step))

    def to_far(step, nothing):
        put_state(gathered(step), far_out, far_out_meta, step)
        start(far_copies(step))
        return nothing

    lax.fori_loop(0, far - 1, to_far, 0)
    state = gathered(far - 1)
    state = merge(
        state, new_state(q_ref[me], qr_ref[me], new_lat_ref[...], new_key_ref[...], tokens)
    )

    def take_far(step, carried):
        landed(far_copies(step))
        return merge(carried, get_state(far_in, far_in_meta, step))

    top, total, acc = lax.fori_loop(0, far - 1, take_far, state)
    out_ref[...] = (acc / total).astype(out_ref.dtype)

    def sent(make, count):
        def step_of(step, nothing):
            for copy in make(step):
                copy.wait_send()
            return nothing

        lax.fori_loop(0, count, step_of, 0)

    sent(core_copies, 2 * far)
    sent(pair_copies, far)
    sent(far_copies, far - 1)


def shards(q_latent, q_rope, cache_latent, cache_rope, new_latent, new_rope, removed):
    devices = lax.axis_size("ctx")
    my_index = lax.axis_index("ctx")
    local_blocks, block_rows, lat_width = cache_latent.shape
    head_count, tokens = (q_latent.shape[0], q_latent.shape[1])
    rope_width = new_rope.shape[1]
    own_heads = head_count // devices
    own_count = own_heads * tokens
    total_blocks = local_blocks * devices
    far = devices // 4
    kept_block, drop_before, kept_rows = span_info(removed, total_blocks, block_rows)
    first_block = my_index * local_blocks
    kept_mine = lax.dynamic_slice_in_dim(kept_block, first_block, local_blocks)
    drop_mine = lax.dynamic_slice_in_dim(drop_before, first_block, local_blocks)
    cosine, sine_part = turn_angles(-drop_mine, rope_width)
    cache_keys = rotate_middle(
        cache_rope.astype(jnp.float32), cosine[:, :, None], sine_part[:, :, None]
    ).astype(jnp.bfloat16)
    key_columns = jnp.transpose(cache_keys, (1, 0, 2)).reshape(rope_width, local_blocks * block_rows)
    positions = kept_rows + jnp.arange(tokens, dtype=jnp.int32)
    query_cos, query_sin = turn_angles(positions, rope_width)
    queries_rope = rotate_last(
        q_rope.reshape(head_count, tokens, rope_width).astype(jnp.float32), query_cos, query_sin
    )
    queries_rope = queries_rope.astype(jnp.bfloat16).reshape(devices, own_count, rope_width)
    new_keys = rotate_last(new_rope.astype(jnp.float32), query_cos, query_sin).astype(jnp.bfloat16)
    query_rows = q_latent.reshape(devices, own_count, lat_width)
    meta_rows = -(-own_count // 128) * 128

    def room(slots):
        return [pltpu.VMEM((slots, own_count, lat_width), jnp.int16)] * 2 + [
            pltpu.VMEM((slots, 8, meta_rows), jnp.float32)
        ] * 2

    vmem = pl.BlockSpec(memory_space=pltpu.VMEM)
    rows = head_count * tokens
    keys = local_blocks * block_rows
    attended = pl.pallas_call(
        lambda *refs: exchange_kernel(far, tokens, *refs),
        out_shape=jax.ShapeDtypeStruct((own_count, lat_width), jnp.bfloat16),
        in_specs=[vmem] * 4 + [pl.BlockSpec(memory_space=pltpu.SMEM)] + [vmem] * 2,
        out_specs=vmem,
        scratch_shapes=room(2 * far) + room(far) + room(far - 1) + [
            pltpu.SemaphoreType.DMA((4, 2 * far)),
            pltpu.SemaphoreType.DMA((4, far)),
            pltpu.SemaphoreType.DMA((4, far - 1)),
        ],
        compiler_params=pltpu.CompilerParams(
            collective_id=0, has_side_effects=True, vmem_limit_bytes=48 * 1024 * 1024
        ),
        cost_estimate=pl.CostEstimate(
            flops=2 * rows * keys * (2 * lat_width + rope_width),
            bytes_accessed=2 * (rows + keys) * (lat_width + rope_width),
            transcendentals=rows * keys,
        ),
    )(
        query_rows, queries_rope, cache_latent, key_columns, kept_mine.astype(jnp.int32),
        new_latent, new_keys,
    )
    return attended.reshape(own_heads, tokens, lat_width)


def solution(mesh):
    in_specs = (
        P(None, "req", None),
        P(None, "req"),
        P(("req", "ctx"), None, None),
        P(("req", "ctx"), None, None),
        P("req", None),
        P("req", None),
        P("req", None),
    )
    out_specs = P("ctx", "req", None)
    return jax.shard_map(shards, mesh=mesh, in_specs=in_specs, out_specs=out_specs, check_vma=False)
```

```python
import jax
import jax.numpy as jnp
import numpy as np
from jax import lax
from jax.experimental import pallas as pl
from jax.experimental.pallas import tpu as pltpu
from jax.sharding import PartitionSpec as P

floor_value = -1e30
score_scale = 192.0 ** (-0.5)


def rope_tables(rope_width):
    halves = rope_width // 2
    frequencies = 10000.0 ** (-2.0 * np.arange(halves) / rope_width)
    coarse = np.mod(4096.0 * frequencies, 2.0 * np.pi)
    middle = np.mod(64.0 * frequencies, 2.0 * np.pi)
    return (
        jnp.asarray(frequencies, jnp.float32),
        jnp.asarray(coarse, jnp.float32),
        jnp.asarray(middle, jnp.float32),
    )


def turn_angles(shift_rows, rope_width):
    frequencies, coarse, middle = rope_tables(rope_width)
    magnitude = jnp.abs(shift_rows)
    signed = jnp.where(shift_rows < 0, -1.0, 1.0).astype(jnp.float32)
    upper_part = (magnitude // 4096).astype(jnp.float32)[..., None]
    centre_part = (magnitude // 64 % 64).astype(jnp.float32)[..., None]
    lowest_part = (magnitude % 64).astype(jnp.float32)[..., None]
    angles = upper_part * coarse + centre_part * middle + lowest_part * frequencies
    return (jnp.cos(angles), signed[..., None] * jnp.sin(angles))


def rotate_last(values, cosine, sine_part):
    halves = values.shape[-1] // 2
    first_half = values[..., :halves]
    second_half = values[..., halves:]
    return jnp.concatenate(
        [
            first_half * cosine - second_half * sine_part,
            first_half * sine_part + second_half * cosine,
        ],
        axis=-1,
    )


def rotate_middle(values, cosine, sine_part):
    halves = values.shape[1] // 2
    first_half = values[:, :halves, :]
    second_half = values[:, halves:, :]
    return jnp.concatenate(
        [
            first_half * cosine - second_half * sine_part,
            first_half * sine_part + second_half * cosine,
        ],
        axis=1,
    )


def span_info(removed, total_blocks, block_rows):
    starts = removed[:, 0]
    finishes = removed[:, 1]
    block_ids = jnp.arange(total_blocks, dtype=jnp.int32)
    inside = (block_ids[:, None] >= starts[None, :]) & (block_ids[:, None] < finishes[None, :])
    kept_block = jnp.logical_not(jnp.any(inside, axis=1))
    drop_before = block_rows * jnp.sum(
        jnp.clip(block_ids[:, None], starts[None, :], finishes[None, :]) - starts[None, :], axis=1
    )
    kept_rows = total_blocks * block_rows - block_rows * jnp.sum(finishes - starts)
    return (kept_block, drop_before, kept_rows)


code_limit = 32767.0
tiny_peak = 1e-30
nt_dims = (((1,), (1,)), ((), ()))


def local_state(q, qr, lat_ref, keys, flag_ref):
    blocks, block_rows, lat_width = lat_ref.shape
    latents = lat_ref[...].reshape(blocks * block_rows, lat_width)
    scores = (
        lax.dot_general(q, latents, nt_dims, preferred_element_type=jnp.float32)
        + jnp.dot(qr, keys, preferred_element_type=jnp.float32)
    ) * score_scale
    lifted, sums, outs = [], [], []
    for b in range(blocks):
        part = scores[:, b * block_rows : (b + 1) * block_rows]
        block_max = jnp.max(part, axis=1, keepdims=True)
        weights = jnp.exp(part - block_max).astype(jnp.bfloat16)
        sums.append(jnp.sum(weights.astype(jnp.float32), axis=1, keepdims=True))
        outs.append(jnp.dot(weights, lat_ref[b], preferred_element_type=jnp.float32))
        lifted.append(jnp.where(flag_ref[b] > 0, block_max, floor_value))
    top = lifted[0]
    for b in range(1, blocks):
        top = jnp.maximum(top, lifted[b])
    total, acc = 0.0, 0.0
    for b in range(blocks):
        factor = jnp.where(flag_ref[b] > 0, jnp.exp(lifted[b] - top), 0.0)
        total = total + sums[b] * factor
        acc = acc + outs[b] * factor
    return top, total, acc


def merge(one, other):
    top = jnp.maximum(one[0], other[0])
    left, right = jnp.exp(one[0] - top), jnp.exp(other[0] - top)
    return top, one[1] * left + other[1] * right, one[2] * left + other[2] * right


def put_state(state, code_ref, meta_ref, slot):
    top, total, acc = state
    rows = acc.shape[0]
    peak = jnp.maximum(jnp.max(jnp.abs(acc), axis=1, keepdims=True), tiny_peak)
    code_ref[slot] = jnp.round(acc * (code_limit / peak)).astype(jnp.int32).astype(jnp.int16)
    lane = lax.broadcasted_iota(jnp.int32, (rows, 128), 1)
    packed = jnp.where(lane == 0, top, jnp.where(lane == 1, total, peak * (1.0 / code_limit)))
    spare = meta_ref.shape[2] - rows
    if spare:
        packed = jnp.concatenate([packed, jnp.zeros((spare, 128), jnp.float32)], axis=0)
    meta_ref[slot] = packed.T[:8]


def get_state(code_ref, meta_ref, slot):
    rows = code_ref.shape[1]
    meta = meta_ref[slot]
    meta = jnp.concatenate([meta, jnp.zeros((120, meta.shape[1]), jnp.float32)], axis=0).T[:rows]
    acc = code_ref[slot].astype(jnp.int32).astype(jnp.float32) * meta[:, 2:3]
    return meta[:, 0:1], meta[:, 1:2], acc


def new_state(q, qr, lat, keys, tokens):
    rows = q.shape[0]
    scores = (
        lax.dot_general(q, lat, nt_dims, preferred_element_type=jnp.float32)
        + lax.dot_general(qr, keys, nt_dims, preferred_element_type=jnp.float32)
    ) * score_scale
    token = lax.broadcasted_iota(jnp.int32, (rows, tokens), 0) % tokens
    causal = lax.broadcasted_iota(jnp.int32, (rows, tokens), 1) <= token
    masked = jnp.where(causal, scores, floor_value)
    top = jnp.max(masked, axis=1, keepdims=True)
    weights = jnp.where(causal, jnp.exp(masked - top), 0.0).astype(jnp.bfloat16)
    total = jnp.sum(weights.astype(jnp.float32), axis=1, keepdims=True)
    return top, total, jnp.dot(weights, lat, preferred_element_type=jnp.float32)


def half_of(state, second, rows):
    return tuple(jnp.where(second, part[rows:], part[:rows]) for part in state)


def exchange_kernel(
    far, tokens, q_ref, qr_ref, lat_ref, key_ref, flag_ref, new_lat_ref, new_key_ref, out_ref,
    core_out, core_in, core_out_meta, core_in_meta,
    pair_out, pair_in, pair_out_meta, pair_in_meta,
    far_out, far_in, far_out_meta, far_in_meta,
    q_buf, held_acc, held_rows,
    core_sems, pair_sems, far_sems, q_sems,
):
    own = out_ref.shape[0]
    me = lax.axis_index("ctx")
    core, pair, place = me % 2, (me // 2) % 2, me // 4

    def index_of(place_id, pair_id, core_id):
        return (place_id * 2 + pair_id) * 2 + core_id

    def place_at(step):
        return (place + 1 + step) % far

    def chip_at(step):
        pair_id = (pair + 1 + step // far) % 2
        return place_at(step % far) * 2 + pair_id

    def q_copy(step):
        return pltpu.make_async_copy(q_ref.at[chip_at(step)], q_buf.at[step], q_sems.at[step])

    def fetch(step, nothing):
        q_copy(step).start()
        return nothing

    lax.fori_loop(0, 2 * far, fetch, 0)
    sibling = index_of(place, pair, 1 - core)
    partner = index_of(place, 1 - pair, core)
    barrier = pltpu.get_barrier_semaphore()
    for other in [sibling, partner]:
        pl.semaphore_signal(barrier, 1, device_id={"ctx": other})

    def greet(step, nothing):
        pl.semaphore_signal(barrier, 1, device_id={"ctx": index_of(place_at(step), pair, core)})
        return nothing

    lax.fori_loop(0, far - 1, greet, 0)
    pl.semaphore_wait(barrier, far + 1)

    def copies(source, landing, source_meta, landing_meta, sems, slot, target):
        return [
            pltpu.make_async_remote_copy(
                src_ref=a.at[slot],
                dst_ref=b.at[slot],
                send_sem=sems.at[2 * kind, slot],
                recv_sem=sems.at[2 * kind + 1, slot],
                device_id={"ctx": target},
            )
            for kind, (a, b) in enumerate([(source, landing), (source_meta, landing_meta)])
        ]

    def core_copies(slot):
        return copies(core_out, core_in, core_out_meta, core_in_meta, core_sems, slot, sibling)

    def pair_copies(slot):
        return copies(pair_out, pair_in, pair_out_meta, pair_in_meta, pair_sems, slot, partner)

    def far_copies(slot):
        target = index_of(place_at(slot), pair, core)
        return copies(far_out, far_in, far_out_meta, far_in_meta, far_sems, slot, target)

    def start(both):
        for copy in both:
            copy.start()

    def landed(both):
        for copy in both:
            copy.wait_recv()

    def hold(state, slot):
        top, total, acc = state
        lane = lax.broadcasted_iota(jnp.int32, (own, 128), 1)
        held_rows[slot] = jnp.where(lane == 0, top, total)
        held_acc[slot] = acc

    def with_sibling(slot):
        rows = held_rows[slot]
        state = rows[:, 0:1], rows[:, 1:2], held_acc[slot]
        landed(core_copies(slot))
        return merge(state, get_state(core_in, core_in_meta, slot))

    def chip_step(step, nothing):
        q_copy(step).wait()
        states = local_state(q_buf[step], qr_ref[chip_at(step)], lat_ref, key_ref[...], flag_ref)
        put_state(half_of(states, core == 0, own), core_out, core_out_meta, step)
        start(core_copies(step))
        hold(half_of(states, core == 1, own), step)

        @pl.when((step >= 1) & (step <= far))
        def to_pair():
            put_state(with_sibling(step - 1), pair_out, pair_out_meta, step - 1)
            start(pair_copies(step - 1))

        return nothing

    lax.fori_loop(0, 2 * far, chip_step, 0)
    last = 2 * far - 1
    fresh = new_state(q_buf[last], qr_ref[chip_at(last)], new_lat_ref[...], new_key_ref[...], tokens)
    fresh = half_of(fresh, core == 1, own)

    def gathered(step):
        state = with_sibling(far + step)
        landed(pair_copies(step))
        return merge(state, get_state(pair_in, pair_in_meta, step))

    def to_far(step, nothing):
        put_state(gathered(step), far_out, far_out_meta, step)
        start(far_copies(step))
        return nothing

    lax.fori_loop(0, far - 1, to_far, 0)
    state = merge(gathered(far - 1), fresh)

    def take_far(step, carried):
        landed(far_copies(step))
        return merge(carried, get_state(far_in, far_in_meta, step))

    top, total, acc = lax.fori_loop(0, far - 1, take_far, state)
    out_ref[...] = (acc / total).astype(out_ref.dtype)

    def sent(make, count):
        def step_of(step, nothing):
            for copy in make(step):
                copy.wait_send()
            return nothing

        lax.fori_loop(0, count, step_of, 0)

    sent(core_copies, 2 * far)
    sent(pair_copies, far)
    sent(far_copies, far - 1)


def shards(q_latent, q_rope, cache_latent, cache_rope, new_latent, new_rope, removed):
    devices = lax.axis_size("ctx")
    my_index = lax.axis_index("ctx")
    local_blocks, block_rows, lat_width = cache_latent.shape
    head_count, tokens = (q_latent.shape[0], q_latent.shape[1])
    rope_width = new_rope.shape[1]
    own_heads = head_count // devices
    own_count = own_heads * tokens
    total_blocks = local_blocks * devices
    far = devices // 4
    kept_block, drop_before, kept_rows = span_info(removed, total_blocks, block_rows)
    first_block = my_index * local_blocks
    kept_mine = lax.dynamic_slice_in_dim(kept_block, first_block, local_blocks)
    drop_mine = lax.dynamic_slice_in_dim(drop_before, first_block, local_blocks)
    cosine, sine_part = turn_angles(-drop_mine, rope_width)
    cache_keys = rotate_middle(
        cache_rope.astype(jnp.float32), cosine[:, :, None], sine_part[:, :, None]
    ).astype(jnp.bfloat16)
    key_columns = jnp.transpose(cache_keys, (1, 0, 2)).reshape(rope_width, local_blocks * block_rows)
    positions = kept_rows + jnp.arange(tokens, dtype=jnp.int32)
    query_cos, query_sin = turn_angles(positions, rope_width)
    queries_rope = rotate_last(
        q_rope.reshape(head_count, tokens, rope_width).astype(jnp.float32), query_cos, query_sin
    )
    queries_rope = queries_rope.astype(jnp.bfloat16).reshape(devices // 2, 2 * own_count, rope_width)
    new_keys = rotate_last(new_rope.astype(jnp.float32), query_cos, query_sin).astype(jnp.bfloat16)
    query_rows = q_latent.reshape(devices // 2, 2 * own_count, lat_width)
    meta_rows = -(-own_count // 128) * 128

    def room(slots):
        return [pltpu.VMEM((slots, own_count, lat_width), jnp.int16)] * 2 + [
            pltpu.VMEM((slots, 8, meta_rows), jnp.float32)
        ] * 2

    vmem = pl.BlockSpec(memory_space=pltpu.VMEM)
    rows = head_count * tokens
    keys = local_blocks * block_rows
    attended = pl.pallas_call(
        lambda *refs: exchange_kernel(far, tokens, *refs),
        out_shape=jax.ShapeDtypeStruct((own_count, lat_width), jnp.bfloat16),
        in_specs=[pl.BlockSpec(memory_space=pl.ANY)] + [vmem] * 3 + [pl.BlockSpec(memory_space=pltpu.SMEM)] + [vmem] * 2,
        out_specs=vmem,
        scratch_shapes=room(2 * far) + room(far) + room(far - 1) + [
            pltpu.VMEM((2 * far, 2 * own_count, lat_width), jnp.bfloat16),
            pltpu.VMEM((2 * far, own_count, lat_width), jnp.float32),
            pltpu.VMEM((2 * far, own_count, 128), jnp.float32),
            pltpu.SemaphoreType.DMA((4, 2 * far)),
            pltpu.SemaphoreType.DMA((4, far)),
            pltpu.SemaphoreType.DMA((4, far - 1)),
            pltpu.SemaphoreType.DMA((2 * far,)),
        ],
        compiler_params=pltpu.CompilerParams(
            collective_id=0, has_side_effects=True, vmem_limit_bytes=48 * 1024 * 1024
        ),
        cost_estimate=pl.CostEstimate(
            flops=2 * rows * keys * (2 * lat_width + rope_width),
            bytes_accessed=2 * (rows + keys) * (lat_width + rope_width),
            transcendentals=rows * keys,
        ),
    )(
        query_rows, queries_rope, cache_latent, key_columns, kept_mine.astype(jnp.int32),
        new_latent, new_keys,
    )
    return attended.reshape(own_heads, tokens, lat_width)


def solution(mesh):
    in_specs = (
        P(None, "req", None),
        P(None, "req"),
        P(("req", "ctx"), None, None),
        P(("req", "ctx"), None, None),
        P("req", None),
        P("req", None),
        P("req", None),
    )
    out_specs = P("ctx", "req", None)
    return jax.shard_map(shards, mesh=mesh, in_specs=in_specs, out_specs=out_specs, check_vma=False)
```

```python
import jax
import jax.numpy as jnp
import numpy as np
from jax import lax
from jax.experimental import pallas as pl
from jax.experimental.pallas import tpu as pltpu
from jax.sharding import PartitionSpec as P

floor_value = -1e30
score_scale = 192.0 ** (-0.5)


def rope_tables(rope_width):
    halves = rope_width // 2
    frequencies = 10000.0 ** (-2.0 * np.arange(halves) / rope_width)
    coarse = np.mod(4096.0 * frequencies, 2.0 * np.pi)
    middle = np.mod(64.0 * frequencies, 2.0 * np.pi)
    return (
        jnp.asarray(frequencies, jnp.float32),
        jnp.asarray(coarse, jnp.float32),
        jnp.asarray(middle, jnp.float32),
    )


def turn_angles(shift_rows, rope_width):
    frequencies, coarse, middle = rope_tables(rope_width)
    magnitude = jnp.abs(shift_rows)
    signed = jnp.where(shift_rows < 0, -1.0, 1.0).astype(jnp.float32)
    upper_part = (magnitude // 4096).astype(jnp.float32)[..., None]
    centre_part = (magnitude // 64 % 64).astype(jnp.float32)[..., None]
    lowest_part = (magnitude % 64).astype(jnp.float32)[..., None]
    angles = upper_part * coarse + centre_part * middle + lowest_part * frequencies
    return (jnp.cos(angles), signed[..., None] * jnp.sin(angles))


def rotate_last(values, cosine, sine_part):
    halves = values.shape[-1] // 2
    first_half = values[..., :halves]
    second_half = values[..., halves:]
    return jnp.concatenate(
        [
            first_half * cosine - second_half * sine_part,
            first_half * sine_part + second_half * cosine,
        ],
        axis=-1,
    )


def rotate_middle(values, cosine, sine_part):
    halves = values.shape[1] // 2
    first_half = values[:, :halves, :]
    second_half = values[:, halves:, :]
    return jnp.concatenate(
        [
            first_half * cosine - second_half * sine_part,
            first_half * sine_part + second_half * cosine,
        ],
        axis=1,
    )


def span_info(removed, total_blocks, block_rows):
    starts = removed[:, 0]
    finishes = removed[:, 1]
    block_ids = jnp.arange(total_blocks, dtype=jnp.int32)
    inside = (block_ids[:, None] >= starts[None, :]) & (block_ids[:, None] < finishes[None, :])
    kept_block = jnp.logical_not(jnp.any(inside, axis=1))
    drop_before = block_rows * jnp.sum(
        jnp.clip(block_ids[:, None], starts[None, :], finishes[None, :]) - starts[None, :], axis=1
    )
    kept_rows = total_blocks * block_rows - block_rows * jnp.sum(finishes - starts)
    return (kept_block, drop_before, kept_rows)


code_limit = 32767.0
tiny_peak = 1e-30
nt_dims = (((1,), (1,)), ((), ()))
tn_dims = (((0,), (0,)), ((), ()))


def block_weights(q, qr, lat_ref, keys, flag_ref):
    blocks, block_rows, lat_width = lat_ref.shape
    latents = lat_ref[...].reshape(blocks * block_rows, lat_width)
    scores = (
        lax.dot_general(latents, q, nt_dims, preferred_element_type=jnp.float32)
        + lax.dot_general(keys, qr, nt_dims, preferred_element_type=jnp.float32)
    ) * score_scale
    lifted, sums, weights = [], [], []
    for b in range(blocks):
        part = scores[b * block_rows : (b + 1) * block_rows]
        block_max = jnp.max(part, axis=0, keepdims=True)
        weights.append(jnp.exp(part - block_max).astype(jnp.bfloat16))
        sums.append(jnp.sum(weights[b].astype(jnp.float32), axis=0, keepdims=True))
        lifted.append(jnp.where(flag_ref[b] > 0, block_max, floor_value))
    top = lifted[0]
    for b in range(1, blocks):
        top = jnp.maximum(top, lifted[b])
    factors = [jnp.where(flag_ref[b] > 0, jnp.exp(lifted[b] - top), 0.0) for b in range(blocks)]
    total = sum(sums[b] * factors[b] for b in range(blocks))
    return top, total, weights, factors


def weighted(columns, weights, factors):
    block_rows = weights[0].shape[0]
    return sum(
        jnp.dot(
            columns[:, b * block_rows : (b + 1) * block_rows],
            weights[b],
            preferred_element_type=jnp.float32,
        )
        * factors[b]
        for b in range(len(weights))
    )


def merge(one, other):
    top = jnp.maximum(one[0], other[0])
    left, right = jnp.exp(one[0] - top), jnp.exp(other[0] - top)
    return top, one[1] * left + other[1] * right, one[2] * left + other[2] * right


def put_state(state, code_ref, meta_ref, slot):
    top, total, acc = state
    peak = jnp.maximum(jnp.max(jnp.abs(acc), axis=0, keepdims=True), tiny_peak)
    code_ref[slot] = jnp.round(acc * (code_limit / peak)).astype(jnp.int32).astype(jnp.int16)
    meta_ref[slot, 0:1] = top
    meta_ref[slot, 1:2] = total
    meta_ref[slot, 2:3] = peak * (1.0 / code_limit)


def get_state(code_ref, meta_ref, slot):
    acc = code_ref[slot].astype(jnp.int32).astype(jnp.float32) * meta_ref[slot, 2:3]
    return meta_ref[slot, 0:1], meta_ref[slot, 1:2], acc


def new_state(q, qr, lat, half, keys):
    tokens, rows = lat.shape[0], q.shape[0]
    scores = (
        lax.dot_general(lat, q, nt_dims, preferred_element_type=jnp.float32)
        + lax.dot_general(keys, qr, nt_dims, preferred_element_type=jnp.float32)
    ) * score_scale
    token = lax.broadcasted_iota(jnp.int32, (tokens, rows), 1) % tokens
    causal = lax.broadcasted_iota(jnp.int32, (tokens, rows), 0) <= token
    masked = jnp.where(causal, scores, floor_value)
    top = jnp.max(masked, axis=0, keepdims=True)
    weights = jnp.where(causal, jnp.exp(masked - top), 0.0).astype(jnp.bfloat16)
    total = jnp.sum(weights.astype(jnp.float32), axis=0, keepdims=True)
    return top, total, lax.dot_general(half, weights, tn_dims, preferred_element_type=jnp.float32)


def exchange_kernel(
    far, q_ref, qr_ref, lat_ref, key_ref, flag_ref, new_lat_ref, new_key_ref, out_ref,
    core_out, core_in, core_out_meta, core_in_meta,
    pair_out, pair_in, pair_out_meta, pair_in_meta,
    far_out, far_in, far_out_meta, far_in_meta,
    q_buf, columns, held_acc, held_rows, swap_out, swap_in,
    core_sems, pair_sems, far_sems, q_sems, swap_sems,
):
    own, lat_width = out_ref.shape
    width = lat_width // 2
    me = lax.axis_index("ctx")
    core, pair, place = me % 2, (me // 2) % 2, me // 4

    def index_of(place_id, pair_id, core_id):
        return (place_id * 2 + pair_id) * 2 + core_id

    def place_at(step):
        return (place + 1 + step) % far

    def chip_at(step):
        pair_id = (pair + 1 + step // far) % 2
        return place_at(step % far) * 2 + pair_id

    def q_copy(step):
        return pltpu.make_async_copy(q_ref.at[chip_at(step)], q_buf.at[step], q_sems.at[step])

    def fetch(step, nothing):
        q_copy(step).start()
        return nothing

    lax.fori_loop(0, 2 * far, fetch, 0)
    sibling = index_of(place, pair, 1 - core)
    partner = index_of(place, 1 - pair, core)
    barrier = pltpu.get_barrier_semaphore()
    for other in [sibling, partner]:
        pl.semaphore_signal(barrier, 1, device_id={"ctx": other})

    def greet(step, nothing):
        pl.semaphore_signal(barrier, 1, device_id={"ctx": index_of(place_at(step), pair, core)})
        return nothing

    lax.fori_loop(0, far - 1, greet, 0)
    turned = lat_ref[...].reshape(columns.shape[2], lat_width).T
    columns[0] = turned[:width]
    columns[1] = turned[width:]
    pl.semaphore_wait(barrier, far + 1)

    def copies(source, landing, source_meta, landing_meta, sems, slot, target):
        return [
            pltpu.make_async_remote_copy(
                src_ref=a.at[slot],
                dst_ref=b.at[slot],
                send_sem=sems.at[2 * kind, slot],
                recv_sem=sems.at[2 * kind + 1, slot],
                device_id={"ctx": target},
            )
            for kind, (a, b) in enumerate([(source, landing), (source_meta, landing_meta)])
        ]

    def core_copies(slot):
        return copies(core_out, core_in, core_out_meta, core_in_meta, core_sems, slot, sibling)

    def pair_copies(slot):
        return copies(pair_out, pair_in, pair_out_meta, pair_in_meta, pair_sems, slot, partner)

    def far_copies(slot):
        target = index_of(place_at(slot), pair, core)
        return copies(far_out, far_in, far_out_meta, far_in_meta, far_sems, slot, target)

    def start(both):
        for copy in both:
            copy.start()

    def landed(both):
        for copy in both:
            copy.wait_recv()

    def with_sibling(slot):
        state = held_rows[slot, 0:1], held_rows[slot, 1:2], held_acc[slot]
        landed(core_copies(slot))
        return merge(state, get_state(core_in, core_in_meta, slot))

    def gathered(step):
        state = with_sibling(far + step)
        landed(pair_copies(step))
        return merge(state, get_state(pair_in, pair_in_meta, step))

    def chip_step(step, nothing):
        q_copy(step).wait()
        top, total, weights, factors = block_weights(
            q_buf[step], qr_ref[chip_at(step)], lat_ref, key_ref[...], flag_ref
        )
        theirs = weighted(columns[1 - core], weights, factors)
        put_state((top, total, theirs), core_out, core_out_meta, step)
        start(core_copies(step))
        held_rows[step, 0:1] = top
        held_rows[step, 1:2] = total
        held_acc[step] = weighted(columns[core], weights, factors)

        @pl.when((step >= 1) & (step <= far))
        def to_pair():
            put_state(with_sibling(step - 1), pair_out, pair_out_meta, step - 1)
            start(pair_copies(step - 1))

        @pl.when(step > far)
        def to_far():
            put_state(gathered(step - 1 - far), far_out, far_out_meta, step - 1 - far)
            start(far_copies(step - 1 - far))

        return nothing

    lax.fori_loop(0, 2 * far, chip_step, 0)
    last = 2 * far - 1
    half = jnp.where(core == 0, new_lat_ref[:, :width], new_lat_ref[:, width:])
    fresh = new_state(q_buf[last], qr_ref[chip_at(last)], new_lat_ref[...], half, new_key_ref[...])
    state = merge(gathered(far - 1), fresh)

    def take_far(step, carried):
        landed(far_copies(step))
        return merge(carried, get_state(far_in, far_in_meta, step))

    top, total, acc = lax.fori_loop(0, far - 1, take_far, state)
    done = acc / total
    spare = -done.shape[1] % 128
    if spare:
        done = jnp.concatenate([done, jnp.zeros((width, spare), jnp.float32)], axis=1)
    done = done.T
    first, second = done[:own], done[own : 2 * own]
    swap_out[...] = jnp.where(core == 0, second, first).astype(out_ref.dtype)
    swap = pltpu.make_async_remote_copy(
        src_ref=swap_out,
        dst_ref=swap_in,
        send_sem=swap_sems.at[0],
        recv_sem=swap_sems.at[1],
        device_id={"ctx": sibling},
    )
    swap.start()
    kept = jnp.where(core == 0, first, second)

    def sent(make, count):
        def step_of(step, nothing):
            for copy in make(step):
                copy.wait_send()
            return nothing

        lax.fori_loop(0, count, step_of, 0)

    sent(core_copies, 2 * far)
    sent(pair_copies, far)
    sent(far_copies, far - 1)
    swap.wait()
    other = swap_in[...].astype(jnp.float32)
    out_ref[:, :width] = jnp.where(core == 0, kept, other).astype(out_ref.dtype)
    out_ref[:, width:] = jnp.where(core == 0, other, kept).astype(out_ref.dtype)


def shards(q_latent, q_rope, cache_latent, cache_rope, new_latent, new_rope, removed):
    devices = lax.axis_size("ctx")
    my_index = lax.axis_index("ctx")
    local_blocks, block_rows, lat_width = cache_latent.shape
    head_count, tokens = (q_latent.shape[0], q_latent.shape[1])
    rope_width = new_rope.shape[1]
    own_heads = head_count // devices
    own_count = own_heads * tokens
    total_blocks = local_blocks * devices
    far = devices // 4
    kept_block, drop_before, kept_rows = span_info(removed, total_blocks, block_rows)
    first_block = my_index * local_blocks
    kept_mine = lax.dynamic_slice_in_dim(kept_block, first_block, local_blocks)
    drop_mine = lax.dynamic_slice_in_dim(drop_before, first_block, local_blocks)
    cosine, sine_part = turn_angles(-drop_mine, rope_width)
    cache_keys = rotate_middle(
        cache_rope.astype(jnp.float32), cosine[:, :, None], sine_part[:, :, None]
    ).astype(jnp.bfloat16)
    key_rows = jnp.transpose(cache_keys, (0, 2, 1)).reshape(local_blocks * block_rows, rope_width)
    positions = kept_rows + jnp.arange(tokens, dtype=jnp.int32)
    query_cos, query_sin = turn_angles(positions, rope_width)
    queries_rope = rotate_last(
        q_rope.reshape(head_count, tokens, rope_width).astype(jnp.float32), query_cos, query_sin
    )
    queries_rope = queries_rope.astype(jnp.bfloat16).reshape(devices // 2, 2 * own_count, rope_width)
    new_keys = rotate_last(new_rope.astype(jnp.float32), query_cos, query_sin).astype(jnp.bfloat16)
    query_rows = q_latent.reshape(devices // 2, 2 * own_count, lat_width)
    chip_rows = 2 * own_count
    width = lat_width // 2

    def room(slots):
        return [pltpu.VMEM((slots, width, chip_rows), jnp.int16)] * 2 + [
            pltpu.VMEM((slots, 8, chip_rows), jnp.float32)
        ] * 2

    vmem = pl.BlockSpec(memory_space=pltpu.VMEM)
    rows = head_count * tokens
    keys = local_blocks * block_rows
    attended = pl.pallas_call(
        lambda *refs: exchange_kernel(far, *refs),
        out_shape=jax.ShapeDtypeStruct((own_count, lat_width), jnp.bfloat16),
        in_specs=[pl.BlockSpec(memory_space=pl.ANY)] + [vmem] * 3 + [pl.BlockSpec(memory_space=pltpu.SMEM)] + [vmem] * 2,
        out_specs=vmem,
        scratch_shapes=room(2 * far) + room(far) + room(far - 1) + [
            pltpu.VMEM((2 * far, chip_rows, lat_width), jnp.bfloat16),
            pltpu.VMEM((2, width, keys), jnp.bfloat16),
            pltpu.VMEM((2 * far, width, chip_rows), jnp.float32),
            pltpu.VMEM((2 * far, 8, chip_rows), jnp.float32),
            pltpu.VMEM((own_count, width), jnp.bfloat16),
            pltpu.VMEM((own_count, width), jnp.bfloat16),
            pltpu.SemaphoreType.DMA((4, 2 * far)),
            pltpu.SemaphoreType.DMA((4, far)),
            pltpu.SemaphoreType.DMA((4, far - 1)),
            pltpu.SemaphoreType.DMA((2 * far,)),
            pltpu.SemaphoreType.DMA((2,)),
        ],
        compiler_params=pltpu.CompilerParams(
            collective_id=0, has_side_effects=True, vmem_limit_bytes=60 * 1024 * 1024
        ),
        cost_estimate=pl.CostEstimate(
            flops=2 * rows * keys * (2 * lat_width + rope_width),
            bytes_accessed=2 * (rows + keys) * (lat_width + rope_width),
            transcendentals=rows * keys,
        ),
    )(
        query_rows, queries_rope, cache_latent, key_rows, kept_mine.astype(jnp.int32),
        new_latent, new_keys,
    )
    return attended.reshape(own_heads, tokens, lat_width)


def solution(mesh):
    in_specs = (
        P(None, "req", None),
        P(None, "req"),
        P(("req", "ctx"), None, None),
        P(("req", "ctx"), None, None),
        P("req", None),
        P("req", None),
        P("req", None),
    )
    out_specs = P("ctx", "req", None)
    return jax.shard_map(shards, mesh=mesh, in_specs=in_specs, out_specs=out_specs, check_vma=False)
```

```python
import jax
import jax.numpy as jnp
import numpy as np
from jax import lax
from jax.experimental import pallas as pl
from jax.experimental.pallas import tpu as pltpu
from jax.sharding import PartitionSpec as P

floor_value = -1e30
score_scale = 192.0 ** (-0.5)


def rope_tables(rope_width):
    halves = rope_width // 2
    frequencies = 10000.0 ** (-2.0 * np.arange(halves) / rope_width)
    coarse = np.mod(4096.0 * frequencies, 2.0 * np.pi)
    middle = np.mod(64.0 * frequencies, 2.0 * np.pi)
    tables = np.zeros((halves + 8, 128), np.float32)
    for digit, table in enumerate([coarse, middle, frequencies]):
        tables[:halves, digit] = table
        tables[halves + digit] = np.tile(table, 128 // halves)
    return tables


def angles_of(rows, coarse, middle, lowest):
    upper_part = (rows >> 12).astype(jnp.float32)
    centre_part = ((rows >> 6) & 63).astype(jnp.float32)
    lowest_part = (rows & 63).astype(jnp.float32)
    return upper_part * coarse + centre_part * middle + lowest_part * lowest


def span_scalars(removed_ref, first_block, local_blocks, total_blocks, block_rows):
    inside = [0] * local_blocks
    drops = [0] * local_blocks
    gone = 0
    for span in range(removed_ref.shape[0]):
        first, last = removed_ref[span, 0], removed_ref[span, 1]
        gone = gone + (last - first)
        for b in range(local_blocks):
            block = first_block + b
            inside[b] = inside[b] + jnp.where((block >= first) & (block < last), 1, 0)
            drops[b] = drops[b] + jnp.minimum(jnp.maximum(block, first), last) - first
    return inside, [block_rows * drop for drop in drops], block_rows * (total_blocks - gone)


def turn_slab(slab, cosine, signed_sine, rope_width):
    halves = rope_width // 2
    lane = lax.broadcasted_iota(jnp.int32, slab.shape, 1)
    swapped = jnp.where(
        lane % rope_width < halves, pltpu.roll(slab, 128 - halves, 1), pltpu.roll(slab, halves, 1)
    )
    return slab * cosine + swapped * signed_sine


code_limit = 32767.0
tiny_peak = 1e-30
nt_dims = (((1,), (1,)), ((), ()))
tn_dims = (((0,), (0,)), ((), ()))


def block_weights(q, qr, lat_ref, keys, inside):
    blocks, block_rows, lat_width = lat_ref.shape
    latents = lat_ref[...].reshape(blocks * block_rows, lat_width)
    scores = (
        lax.dot_general(latents, q, nt_dims, preferred_element_type=jnp.float32)
        + lax.dot_general(keys, qr, nt_dims, preferred_element_type=jnp.float32)
    ) * score_scale
    lifted, sums, weights = [], [], []
    for b in range(blocks):
        part = scores[b * block_rows : (b + 1) * block_rows]
        block_max = jnp.max(part, axis=0, keepdims=True)
        weights.append(jnp.exp(part - block_max).astype(jnp.bfloat16))
        sums.append(jnp.sum(weights[b].astype(jnp.float32), axis=0, keepdims=True))
        lifted.append(jnp.where(inside[b] == 0, block_max, floor_value))
    top = lifted[0]
    for b in range(1, blocks):
        top = jnp.maximum(top, lifted[b])
    factors = [jnp.where(inside[b] == 0, jnp.exp(lifted[b] - top), 0.0) for b in range(blocks)]
    total = sum(sums[b] * factors[b] for b in range(blocks))
    return top, total, weights, factors


def weighted(columns, weights, factors):
    block_rows = weights[0].shape[0]
    return sum(
        jnp.dot(
            columns[:, b * block_rows : (b + 1) * block_rows],
            weights[b],
            preferred_element_type=jnp.float32,
        )
        * factors[b]
        for b in range(len(weights))
    )


def merge(one, other):
    top = jnp.maximum(one[0], other[0])
    left, right = jnp.exp(one[0] - top), jnp.exp(other[0] - top)
    return top, one[1] * left + other[1] * right, one[2] * left + other[2] * right


def put_state(state, code_ref, meta_ref, slot):
    top, total, acc = state
    peak = jnp.maximum(jnp.max(jnp.abs(acc), axis=0, keepdims=True), tiny_peak)
    code_ref[slot] = jnp.round(acc * (code_limit / peak)).astype(jnp.int32).astype(jnp.int16)
    meta_ref[slot, 0:1] = top
    meta_ref[slot, 1:2] = total
    meta_ref[slot, 2:3] = peak * (1.0 / code_limit)


def get_state(code_ref, meta_ref, slot):
    acc = code_ref[slot].astype(jnp.int32).astype(jnp.float32) * meta_ref[slot, 2:3]
    return meta_ref[slot, 0:1], meta_ref[slot, 1:2], acc


def new_state(q, qr, lat, half, keys):
    tokens, rows = lat.shape[0], q.shape[0]
    scores = (
        lax.dot_general(lat, q, nt_dims, preferred_element_type=jnp.float32)
        + lax.dot_general(keys, qr, nt_dims, preferred_element_type=jnp.float32)
    ) * score_scale
    token = lax.broadcasted_iota(jnp.int32, (tokens, rows), 1) % tokens
    causal = lax.broadcasted_iota(jnp.int32, (tokens, rows), 0) <= token
    masked = jnp.where(causal, scores, floor_value)
    top = jnp.max(masked, axis=0, keepdims=True)
    weights = jnp.where(causal, jnp.exp(masked - top), 0.0).astype(jnp.bfloat16)
    total = jnp.sum(weights.astype(jnp.float32), axis=0, keepdims=True)
    return top, total, lax.dot_general(half, weights, tn_dims, preferred_element_type=jnp.float32)


def exchange_kernel(
    far, q_ref, rope_ref, lat_ref, cache_rope_ref, new_lat_ref, new_rope_ref, removed_ref, table_ref, out_ref,
    core_out, core_in, core_out_meta, core_in_meta,
    pair_out, pair_in, pair_out_meta, pair_in_meta,
    far_out, far_in, far_out_meta, far_in_meta,
    q_buf, columns, held_acc, held_rows, swap_out, swap_in,
    key_rows, new_keys, slab_cos, slab_sin, pick,
    core_sems, pair_sems, far_sems, q_sems, swap_sems,
):
    own, lat_width = out_ref.shape
    width = lat_width // 2
    me = lax.axis_index("ctx")
    core, pair, place = me % 2, (me // 2) % 2, me // 4

    def index_of(place_id, pair_id, core_id):
        return (place_id * 2 + pair_id) * 2 + core_id

    def place_at(step):
        return (place + 1 + step) % far

    def chip_at(step):
        pair_id = (pair + 1 + step // far) % 2
        return place_at(step % far) * 2 + pair_id

    def q_copy(step):
        return pltpu.make_async_copy(q_ref.at[chip_at(step)], q_buf.at[step], q_sems.at[step])

    def fetch(step, nothing):
        q_copy(step).start()
        return nothing

    lax.fori_loop(0, 2 * far, fetch, 0)
    sibling = index_of(place, pair, 1 - core)
    partner = index_of(place, 1 - pair, core)
    barrier = pltpu.get_barrier_semaphore()
    for other in [sibling, partner]:
        pl.semaphore_signal(barrier, 1, device_id={"ctx": other})

    def greet(step, nothing):
        pl.semaphore_signal(barrier, 1, device_id={"ctx": index_of(place_at(step), pair, core)})
        return nothing

    lax.fori_loop(0, far - 1, greet, 0)
    blocks, block_rows = lat_ref.shape[:2]
    tokens, rope_width = new_rope_ref.shape
    halves, group = rope_width // 2, 128 // rope_width
    slabs = tokens // group
    turned = lat_ref[...].reshape(columns.shape[2], lat_width).T
    columns[0] = turned[:width]
    columns[1] = turned[width:]
    inside, drops, kept_rows = span_scalars(
        removed_ref, me * blocks, blocks, blocks * 4 * far, block_rows
    )
    along = [table_ref[halves + digit : halves + digit + 1] for digit in range(3)]
    down = [table_ref[:halves, digit : digit + 1] for digit in range(3)]

    def signed(sine):
        lane = lax.broadcasted_iota(jnp.int32, sine.shape, 1)
        return jnp.where(lane % rope_width < halves, -sine, sine)

    row = lax.broadcasted_iota(jnp.int32, (slabs, 128), 0)
    lane = lax.broadcasted_iota(jnp.int32, (slabs, 128), 1)
    angles = angles_of(kept_rows + row * group + lane // rope_width, *along)
    slab_cos[...] = jnp.cos(angles)
    slab_sin[...] = signed(jnp.sin(angles))
    angles = angles_of(kept_rows + lax.broadcasted_iota(jnp.int32, (tokens, 128), 0), *along)
    fresh_rope = jnp.concatenate([new_rope_ref[...].astype(jnp.float32)] * group, axis=1)
    new_keys[...] = turn_slab(
        fresh_rope, jnp.cos(angles), signed(jnp.sin(angles)), rope_width
    ).astype(jnp.bfloat16)
    lane = lax.broadcasted_iota(jnp.int32, (halves, 128), 1)
    dropped = jnp.zeros((halves, 128), jnp.int32)
    for b in range(blocks):
        dropped = jnp.where(lane == b, drops[b], dropped)
    angles = angles_of(dropped, *down)
    cosine, sine = jnp.cos(angles), -jnp.sin(angles)
    for b in range(blocks):
        c, s = cosine[:, b : b + 1], sine[:, b : b + 1]
        first = cache_rope_ref[b, :halves].astype(jnp.float32)
        second = cache_rope_ref[b, halves:].astype(jnp.float32)
        keys = jnp.concatenate([first * c - second * s, first * s + second * c] * group, axis=0)
        key_rows[b * block_rows : (b + 1) * block_rows] = keys.T.astype(jnp.bfloat16)
    heads = rope_ref.shape[1]
    head_rows = pick.shape[1] // slabs
    row = lax.broadcasted_iota(jnp.int32, pick.shape, 0)
    column = lax.broadcasted_iota(jnp.int32, pick.shape, 1)
    chosen = (row % tokens) // group * head_rows + row // tokens
    pick[...] = jnp.where(column == chosen, 1.0, 0.0).astype(jnp.bfloat16)

    def rope_rows(chip):
        values = rope_ref[chip].astype(jnp.float32)
        if head_rows > heads:
            spare = jnp.zeros((head_rows - heads, values.shape[1]), jnp.float32)
            values = jnp.concatenate([values, spare], axis=0)
        turned = [
            turn_slab(
                values[:, j * 128 : (j + 1) * 128],
                slab_cos[j : j + 1],
                slab_sin[j : j + 1],
                rope_width,
            )
            for j in range(slabs)
        ]
        stacked = jnp.concatenate(turned, axis=0).astype(jnp.bfloat16)
        rows = jnp.dot(pick[...], stacked, preferred_element_type=jnp.float32)
        row = lax.broadcasted_iota(jnp.int32, rows.shape, 0)
        lane = lax.broadcasted_iota(jnp.int32, rows.shape, 1)
        own_lanes = lane // rope_width == row % tokens % group
        return jnp.where(own_lanes, rows, 0.0).astype(jnp.bfloat16)

    pl.semaphore_wait(barrier, far + 1)

    def copies(source, landing, source_meta, landing_meta, sems, slot, target):
        return [
            pltpu.make_async_remote_copy(
                src_ref=a.at[slot],
                dst_ref=b.at[slot],
                send_sem=sems.at[2 * kind, slot],
                recv_sem=sems.at[2 * kind + 1, slot],
                device_id={"ctx": target},
            )
            for kind, (a, b) in enumerate([(source, landing), (source_meta, landing_meta)])
        ]

    def core_copies(slot):
        return copies(core_out, core_in, core_out_meta, core_in_meta, core_sems, slot, sibling)

    def pair_copies(slot):
        return copies(pair_out, pair_in, pair_out_meta, pair_in_meta, pair_sems, slot, partner)

    def far_copies(slot):
        target = index_of(place_at(slot), pair, core)
        return copies(far_out, far_in, far_out_meta, far_in_meta, far_sems, slot, target)

    def start(both):
        for copy in both:
            copy.start()

    def landed(both):
        for copy in both:
            copy.wait_recv()

    def with_sibling(slot):
        state = held_rows[slot, 0:1], held_rows[slot, 1:2], held_acc[slot]
        landed(core_copies(slot))
        return merge(state, get_state(core_in, core_in_meta, slot))

    def gathered(step):
        state = with_sibling(far + step)
        landed(pair_copies(step))
        return merge(state, get_state(pair_in, pair_in_meta, step))

    def chip_step(step, nothing):
        q_copy(step).wait()
        top, total, weights, factors = block_weights(
            q_buf[step], rope_rows(chip_at(step)), lat_ref, key_rows[...], inside
        )
        theirs = weighted(columns[1 - core], weights, factors)
        put_state((top, total, theirs), core_out, core_out_meta, step)
        start(core_copies(step))
        held_rows[step, 0:1] = top
        held_rows[step, 1:2] = total
        held_acc[step] = weighted(columns[core], weights, factors)

        @pl.when((step >= 1) & (step <= far))
        def to_pair():
            put_state(with_sibling(step - 1), pair_out, pair_out_meta, step - 1)
            start(pair_copies(step - 1))

        @pl.when(step > far)
        def to_far():
            put_state(gathered(step - 1 - far), far_out, far_out_meta, step - 1 - far)
            start(far_copies(step - 1 - far))

        return nothing

    lax.fori_loop(0, 2 * far, chip_step, 0)
    last = 2 * far - 1
    half = jnp.where(core == 0, new_lat_ref[:, :width], new_lat_ref[:, width:])
    fresh = new_state(
        q_buf[last], rope_rows(chip_at(last)), new_lat_ref[...], half, new_keys[...]
    )
    state = merge(gathered(far - 1), fresh)

    def take_far(step, carried):
        landed(far_copies(step))
        return merge(carried, get_state(far_in, far_in_meta, step))

    top, total, acc = lax.fori_loop(0, far - 1, take_far, state)
    done = acc / total
    spare = -done.shape[1] % 128
    if spare:
        done = jnp.concatenate([done, jnp.zeros((width, spare), jnp.float32)], axis=1)
    done = done.T
    first, second = done[:own], done[own : 2 * own]
    swap_out[...] = jnp.where(core == 0, second, first).astype(out_ref.dtype)
    swap = pltpu.make_async_remote_copy(
        src_ref=swap_out,
        dst_ref=swap_in,
        send_sem=swap_sems.at[0],
        recv_sem=swap_sems.at[1],
        device_id={"ctx": sibling},
    )
    swap.start()
    kept = jnp.where(core == 0, first, second)

    def sent(make, count):
        def step_of(step, nothing):
            for copy in make(step):
                copy.wait_send()
            return nothing

        lax.fori_loop(0, count, step_of, 0)

    sent(core_copies, 2 * far)
    sent(pair_copies, far)
    sent(far_copies, far - 1)
    swap.wait()
    other = swap_in[...].astype(jnp.float32)
    out_ref[:, :width] = jnp.where(core == 0, kept, other).astype(out_ref.dtype)
    out_ref[:, width:] = jnp.where(core == 0, other, kept).astype(out_ref.dtype)


def shards(q_latent, q_rope, cache_latent, cache_rope, new_latent, new_rope, removed):
    devices = lax.axis_size("ctx")
    local_blocks, block_rows, lat_width = cache_latent.shape
    head_count, tokens = (q_latent.shape[0], q_latent.shape[1])
    rope_width = new_rope.shape[1]
    own_heads = head_count // devices
    own_count = own_heads * tokens
    far = devices // 4
    chips = devices // 2
    chip_rows = 2 * own_count
    width = lat_width // 2
    rows = head_count * tokens
    keys = local_blocks * block_rows
    slabs = tokens * rope_width // 128
    head_rows = -(-2 * own_heads // 8) * 8

    def room(slots):
        return [pltpu.VMEM((slots, width, chip_rows), jnp.int16)] * 2 + [
            pltpu.VMEM((slots, 8, chip_rows), jnp.float32)
        ] * 2

    vmem = pl.BlockSpec(memory_space=pltpu.VMEM)
    attended = pl.pallas_call(
        lambda *refs: exchange_kernel(far, *refs),
        out_shape=jax.ShapeDtypeStruct((own_count, lat_width), jnp.bfloat16),
        in_specs=[pl.BlockSpec(memory_space=pl.ANY)]
        + [vmem] * 5
        + [pl.BlockSpec(memory_space=pltpu.SMEM), vmem],
        out_specs=vmem,
        scratch_shapes=room(2 * far) + room(far) + room(far - 1) + [
            pltpu.VMEM((2 * far, chip_rows, lat_width), jnp.bfloat16),
            pltpu.VMEM((2, width, keys), jnp.bfloat16),
            pltpu.VMEM((2 * far, width, chip_rows), jnp.float32),
            pltpu.VMEM((2 * far, 8, chip_rows), jnp.float32),
            pltpu.VMEM((own_count, width), jnp.bfloat16),
            pltpu.VMEM((own_count, width), jnp.bfloat16),
            pltpu.VMEM((keys, 128), jnp.bfloat16),
            pltpu.VMEM((tokens, 128), jnp.bfloat16),
            pltpu.VMEM((slabs, 128), jnp.float32),
            pltpu.VMEM((slabs, 128), jnp.float32),
            pltpu.VMEM((chip_rows, slabs * head_rows), jnp.bfloat16),
            pltpu.SemaphoreType.DMA((4, 2 * far)),
            pltpu.SemaphoreType.DMA((4, far)),
            pltpu.SemaphoreType.DMA((4, far - 1)),
            pltpu.SemaphoreType.DMA((2 * far,)),
            pltpu.SemaphoreType.DMA((2,)),
        ],
        compiler_params=pltpu.CompilerParams(
            collective_id=0, has_side_effects=True, vmem_limit_bytes=60 * 1024 * 1024
        ),
        cost_estimate=pl.CostEstimate(
            flops=2 * rows * keys * (2 * lat_width + rope_width),
            bytes_accessed=2 * (rows + keys) * (lat_width + rope_width),
            transcendentals=rows * keys,
        ),
    )(
        q_latent.reshape(chips, chip_rows, lat_width),
        q_rope.reshape(chips, 2 * own_heads, tokens * rope_width),
        cache_latent, cache_rope, new_latent, new_rope, removed,
        jnp.asarray(rope_tables(rope_width)),
    )
    return attended.reshape(own_heads, tokens, lat_width)


def solution(mesh):
    in_specs = (
        P(None, "req", None),
        P(None, "req"),
        P(("req", "ctx"), None, None),
        P(("req", "ctx"), None, None),
        P("req", None),
        P("req", None),
        P("req", None),
    )
    out_specs = P("ctx", "req", None)
    return jax.shard_map(shards, mesh=mesh, in_specs=in_specs, out_specs=out_specs, check_vma=False)
```

```python
import jax
import jax.numpy as jnp
import numpy as np
from jax import lax
from jax.experimental import pallas as pl
from jax.experimental.pallas import tpu as pltpu
from jax.sharding import PartitionSpec as P

floor_value = -1e30
score_scale = 192.0 ** (-0.5)


def rope_tables(rope_width):
    halves = rope_width // 2
    frequencies = 10000.0 ** (-2.0 * np.arange(halves) / rope_width)
    coarse = np.mod(4096.0 * frequencies, 2.0 * np.pi)
    middle = np.mod(64.0 * frequencies, 2.0 * np.pi)
    tables = np.zeros((halves + 8, 128), np.float32)
    for digit, table in enumerate([coarse, middle, frequencies]):
        tables[:halves, digit] = table
        tables[halves + digit] = np.tile(table, 128 // halves)
    return tables


def angles_of(rows, coarse, middle, lowest):
    upper_part = (rows >> 12).astype(jnp.float32)
    centre_part = ((rows >> 6) & 63).astype(jnp.float32)
    lowest_part = (rows & 63).astype(jnp.float32)
    return upper_part * coarse + centre_part * middle + lowest_part * lowest


def span_scalars(removed_ref, first_block, local_blocks, total_blocks, block_rows):
    inside = [0] * local_blocks
    drops = [0] * local_blocks
    gone = 0
    for span in range(removed_ref.shape[1]):
        first, last = removed_ref[0, span], removed_ref[1, span]
        gone = gone + (last - first)
        for b in range(local_blocks):
            block = first_block + b
            inside[b] = inside[b] + jnp.where((block >= first) & (block < last), 1, 0)
            drops[b] = drops[b] + jnp.minimum(jnp.maximum(block, first), last) - first
    return inside, [block_rows * drop for drop in drops], block_rows * (total_blocks - gone)


def turn_slab(slab, cosine, signed_sine, rope_width):
    halves = rope_width // 2
    lane = lax.broadcasted_iota(jnp.int32, slab.shape, 1)
    swapped = jnp.where(
        lane % rope_width < halves, pltpu.roll(slab, 128 - halves, 1), pltpu.roll(slab, halves, 1)
    )
    return slab * cosine + swapped * signed_sine


code_limit = 32767.0
exponent_scale = score_scale * 1.4426950408889634
tiny_peak = 1e-30
nt_dims = (((1,), (1,)), ((), ()))
tn_dims = (((0,), (0,)), ((), ()))


def block_weights(q, qr, lat_ref, keys, inside):
    blocks, block_rows, lat_width = lat_ref.shape
    latents = lat_ref[...].reshape(blocks * block_rows, lat_width)
    scores = (
        lax.dot_general(latents, q, nt_dims, preferred_element_type=jnp.float32)
        + lax.dot_general(keys, qr, nt_dims, preferred_element_type=jnp.float32)
    )
    lifted, weights = [], []
    for b in range(blocks):
        part = scores[b * block_rows : (b + 1) * block_rows]
        block_max = jnp.max(part, axis=0, keepdims=True)
        weights.append(jnp.exp2((part - block_max) * exponent_scale).astype(jnp.bfloat16))
        lifted.append(jnp.where(inside[b] == 0, block_max * score_scale, floor_value))
    top = lifted[0]
    for b in range(1, blocks):
        top = jnp.maximum(top, lifted[b])
    factors = [jnp.where(inside[b] == 0, jnp.exp(lifted[b] - top), 0.0) for b in range(blocks)]
    return top, weights, factors


def weighted(columns, weights, factors):
    block_rows = weights[0].shape[0]
    return sum(
        jnp.dot(
            columns[:, b * block_rows : (b + 1) * block_rows],
            weights[b],
            preferred_element_type=jnp.float32,
        )
        * factors[b]
        for b in range(len(weights))
    )


def merge(one, other):
    top = jnp.maximum(one[0], other[0])
    left, right = jnp.exp(one[0] - top), jnp.exp(other[0] - top)
    return top, one[1] * left + other[1] * right, one[2] * left + other[2] * right


def put_state(state, code_ref, meta_ref, slot):
    top, total, acc = state
    peak = jnp.maximum(jnp.max(jnp.abs(acc), axis=0, keepdims=True), tiny_peak)
    code_ref[slot] = jnp.round(acc * (code_limit / peak)).astype(jnp.int32).astype(jnp.int16)
    meta_ref[slot, 0:1] = top
    meta_ref[slot, 1:2] = total
    meta_ref[slot, 2:3] = peak * (1.0 / code_limit)


def get_state(code_ref, meta_ref, slot):
    acc = code_ref[slot].astype(jnp.int32).astype(jnp.float32) * meta_ref[slot, 2:3]
    return meta_ref[slot, 0:1], meta_ref[slot, 1:2], acc


def new_state(q, qr, lat, half, keys):
    tokens, rows = lat.shape[0], q.shape[0]
    scores = (
        lax.dot_general(lat, q, nt_dims, preferred_element_type=jnp.float32)
        + lax.dot_general(keys, qr, nt_dims, preferred_element_type=jnp.float32)
    ) * score_scale
    token = lax.broadcasted_iota(jnp.int32, (tokens, rows), 1) % tokens
    causal = lax.broadcasted_iota(jnp.int32, (tokens, rows), 0) <= token
    masked = jnp.where(causal, scores, floor_value)
    top = jnp.max(masked, axis=0, keepdims=True)
    weights = jnp.where(causal, jnp.exp(masked - top), 0.0).astype(jnp.bfloat16)
    total = jnp.sum(weights.astype(jnp.float32), axis=0, keepdims=True)
    return top, total, lax.dot_general(half, weights, tn_dims, preferred_element_type=jnp.float32)


def exchange_kernel(
    far, q_ref, rope_ref, lat_ref, cache_rope_ref, new_lat_ref, new_rope_ref, removed_ref, table_ref, out_ref,
    core_out, core_in, core_out_meta, core_in_meta,
    pair_out, pair_in, pair_out_meta, pair_in_meta,
    far_out, far_in, far_out_meta, far_in_meta,
    q_buf, columns, held_acc, held_rows, swap_out, swap_in,
    key_rows, new_keys, slab_cos, slab_sin, pick,
    core_sems, pair_sems, far_sems, q_sems, swap_sems,
):
    own, lat_width = out_ref.shape
    width = lat_width // 2
    me = lax.axis_index("ctx")
    core, pair, place = me % 2, (me // 2) % 2, me // 4

    def index_of(place_id, pair_id, core_id):
        return (place_id * 2 + pair_id) * 2 + core_id

    bits = far.bit_length() - 1

    def flipped(bit):
        return (1 - place // 2**bit % 2 * 2) * 2**bit

    def place_at(step):
        apart = far - 1 - step
        return place + sum(flipped(bit) * (apart // 2**bit % 2) for bit in range(bits))

    def next_place(step):
        apart = far - 1 - step
        return place + sum(
            flipped(bit) * jnp.where(apart % 2 ** (bit + 1) == 2**bit, 1, 0) for bit in range(bits)
        )

    def chip_at(step):
        pair_id = (pair + 1 + step // far) % 2
        return place_at(step % far) * 2 + pair_id

    def q_copy(step):
        return pltpu.make_async_copy(q_ref.at[chip_at(step)], q_buf.at[step], q_sems.at[step])

    def fetch(step, nothing):
        q_copy(step).start()
        return nothing

    lax.fori_loop(0, 2 * far, fetch, 0)
    sibling = index_of(place, pair, 1 - core)
    partner = index_of(place, 1 - pair, core)
    barrier = pltpu.get_barrier_semaphore()
    for other in [sibling, partner]:
        pl.semaphore_signal(barrier, 1, device_id={"ctx": other})

    for bit in range(bits):
        other = index_of(place + flipped(bit), pair, core)
        pl.semaphore_signal(barrier, 1, device_id={"ctx": other})
    blocks, block_rows = lat_ref.shape[:2]
    tokens, rope_width = new_rope_ref.shape
    halves, group = rope_width // 2, 128 // rope_width
    slabs = tokens // group
    turned = lat_ref[...].reshape(columns.shape[2], lat_width).T
    columns[0, :width] = turned[:width]
    columns[1, :width] = turned[width:]
    for side in range(2):
        columns[side, width:] = jnp.ones((16, columns.shape[2]), jnp.bfloat16)
    inside, drops, kept_rows = span_scalars(
        removed_ref, me * blocks, blocks, blocks * 4 * far, block_rows
    )
    along = [table_ref[halves + digit : halves + digit + 1] for digit in range(3)]
    down = [table_ref[:halves, digit : digit + 1] for digit in range(3)]

    def signed(sine):
        lane = lax.broadcasted_iota(jnp.int32, sine.shape, 1)
        return jnp.where(lane % rope_width < halves, -sine, sine)

    row = lax.broadcasted_iota(jnp.int32, (slabs, 128), 0)
    lane = lax.broadcasted_iota(jnp.int32, (slabs, 128), 1)
    angles = angles_of(kept_rows + row * group + lane // rope_width, *along)
    slab_cos[...] = jnp.cos(angles)
    slab_sin[...] = signed(jnp.sin(angles))
    angles = angles_of(kept_rows + lax.broadcasted_iota(jnp.int32, (tokens, 128), 0), *along)
    fresh_rope = jnp.concatenate([new_rope_ref[...].astype(jnp.float32)] * group, axis=1)
    new_keys[...] = turn_slab(
        fresh_rope, jnp.cos(angles), signed(jnp.sin(angles)), rope_width
    ).astype(jnp.bfloat16)
    lane = lax.broadcasted_iota(jnp.int32, (halves, 128), 1)
    dropped = jnp.zeros((halves, 128), jnp.int32)
    for b in range(blocks):
        dropped = jnp.where(lane == b, drops[b], dropped)
    angles = angles_of(dropped, *down)
    cosine, sine = jnp.cos(angles), -jnp.sin(angles)
    for b in range(blocks):
        c, s = cosine[:, b : b + 1], sine[:, b : b + 1]
        first = cache_rope_ref[b, :halves].astype(jnp.float32)
        second = cache_rope_ref[b, halves:].astype(jnp.float32)
        keys = jnp.concatenate([first * c - second * s, first * s + second * c] * group, axis=0)
        key_rows[b * block_rows : (b + 1) * block_rows] = keys.T.astype(jnp.bfloat16)
    heads = rope_ref.shape[1]
    head_rows = pick.shape[1] // slabs
    row = lax.broadcasted_iota(jnp.int32, pick.shape, 0)
    column = lax.broadcasted_iota(jnp.int32, pick.shape, 1)
    chosen = (row % tokens) // group * head_rows + row // tokens
    pick[...] = jnp.where(column == chosen, 1.0, 0.0).astype(jnp.bfloat16)

    def rope_rows(chip):
        values = rope_ref[chip].astype(jnp.float32)
        if head_rows > heads:
            spare = jnp.zeros((head_rows - heads, values.shape[1]), jnp.float32)
            values = jnp.concatenate([values, spare], axis=0)
        turned = [
            turn_slab(
                values[:, j * 128 : (j + 1) * 128],
                slab_cos[j : j + 1],
                slab_sin[j : j + 1],
                rope_width,
            )
            for j in range(slabs)
        ]
        stacked = jnp.concatenate(turned, axis=0).astype(jnp.bfloat16)
        rows = jnp.dot(pick[...], stacked, preferred_element_type=jnp.float32)
        row = lax.broadcasted_iota(jnp.int32, rows.shape, 0)
        lane = lax.broadcasted_iota(jnp.int32, rows.shape, 1)
        own_lanes = lane // rope_width == row % tokens % group
        return jnp.where(own_lanes, rows, 0.0).astype(jnp.bfloat16)

    pl.semaphore_wait(barrier, bits + 2)

    def copies(source, landing, source_meta, landing_meta, sems, slot, target):
        return [
            pltpu.make_async_remote_copy(
                src_ref=a.at[slot],
                dst_ref=b.at[slot],
                send_sem=sems.at[2 * kind, slot],
                recv_sem=sems.at[2 * kind + 1, slot],
                device_id={"ctx": target},
            )
            for kind, (a, b) in enumerate([(source, landing), (source_meta, landing_meta)])
        ]

    def core_copies(slot):
        return copies(core_out, core_in, core_out_meta, core_in_meta, core_sems, slot, sibling)

    def pair_copies(slot):
        return copies(pair_out, pair_in, pair_out_meta, pair_in_meta, pair_sems, slot, partner)

    def far_copies(slot):
        target = index_of(next_place(slot), pair, core)
        return copies(far_out, far_in, far_out_meta, far_in_meta, far_sems, slot, target)

    def start(both):
        for copy in both:
            copy.start()

    def landed(both):
        for copy in both:
            copy.wait_recv()

    def put_held(state, slot):
        held_rows[slot, 0:1] = state[0]
        held_rows[slot, 1:2] = state[1]
        held_acc[slot] = state[2]

    def get_held(slot):
        return held_rows[slot, 0:1], held_rows[slot, 1:2], held_acc[slot]

    def with_sibling(slot):
        landed(core_copies(slot))
        return merge(get_held(slot), get_state(core_in, core_in_meta, slot))

    def gather(step):
        state = with_sibling(far + step)
        landed(pair_copies(step))
        put_held(merge(state, get_state(pair_in, pair_in_meta, step)), far + step)
        for bit in range(bits):

            @pl.when((far - 1 - step) % 2 ** (bit + 1) == 0)
            def take_far():
                landed(far_copies(step - 2**bit))
                arrived = get_state(far_in, far_in_meta, step - 2**bit)
                put_held(merge(get_held(far + step), arrived), far + step)

    def to_far(step):
        gather(step)
        put_state(get_held(far + step), far_out, far_out_meta, step)
        start(far_copies(step))

    def chip_step(step, nothing):
        q_copy(step).wait()
        top, weights, factors = block_weights(
            q_buf[step], rope_rows(chip_at(step)), lat_ref, key_rows[...], inside
        )
        theirs = weighted(columns[1 - core], weights, factors)
        total = theirs[width : width + 1]
        put_state((top, total, theirs[:width]), core_out, core_out_meta, step)
        start(core_copies(step))
        put_held((top, total, weighted(columns[core, :width], weights, factors)), step)

        @pl.when((step >= 1) & (step <= far))
        def to_pair():
            put_state(with_sibling(step - 1), pair_out, pair_out_meta, step - 1)
            start(pair_copies(step - 1))

        @pl.when(step > far)
        def onward():
            to_far(step - 1 - far)

        return nothing

    lax.fori_loop(0, 2 * far, chip_step, 0)
    last = 2 * far - 1
    half = jnp.where(core == 0, new_lat_ref[:, :width], new_lat_ref[:, width:])
    fresh = new_state(
        q_buf[last], rope_rows(chip_at(last)), new_lat_ref[...], half, new_keys[...]
    )
    gather(far - 1)

    top, total, acc = merge(get_held(last), fresh)
    done = acc / total
    spare = -done.shape[1] % 128
    if spare:
        done = jnp.concatenate([done, jnp.zeros((width, spare), jnp.float32)], axis=1)
    done = done.T
    first, second = done[:own], done[own : 2 * own]
    swap_out[...] = jnp.where(core == 0, second, first).astype(out_ref.dtype)
    swap = pltpu.make_async_remote_copy(
        src_ref=swap_out,
        dst_ref=swap_in,
        send_sem=swap_sems.at[0],
        recv_sem=swap_sems.at[1],
        device_id={"ctx": sibling},
    )
    swap.start()
    kept = jnp.where(core == 0, first, second)

    def sent(make, count):
        def step_of(step, nothing):
            for copy in make(step):
                copy.wait_send()
            return nothing

        lax.fori_loop(0, count, step_of, 0)

    sent(core_copies, 2 * far)
    sent(pair_copies, far)
    sent(far_copies, far - 1)
    swap.wait()
    other = swap_in[...].astype(jnp.float32)
    out_ref[:, :width] = jnp.where(core == 0, kept, other).astype(out_ref.dtype)
    out_ref[:, width:] = jnp.where(core == 0, other, kept).astype(out_ref.dtype)


def shards(q_latent, q_rope, cache_latent, cache_rope, new_latent, new_rope, removed):
    devices = lax.axis_size("ctx")
    local_blocks, block_rows, lat_width = cache_latent.shape
    head_count, tokens = (q_latent.shape[0], q_latent.shape[1])
    rope_width = new_rope.shape[1]
    own_heads = head_count // devices
    own_count = own_heads * tokens
    far = devices // 4
    chips = devices // 2
    chip_rows = 2 * own_count
    width = lat_width // 2
    rows = head_count * tokens
    keys = local_blocks * block_rows
    slabs = tokens * rope_width // 128
    head_rows = -(-2 * own_heads // 8) * 8

    def room(slots):
        return [pltpu.VMEM((slots, width, chip_rows), jnp.int16)] * 2 + [
            pltpu.VMEM((slots, 8, chip_rows), jnp.float32)
        ] * 2

    vmem = pl.BlockSpec(memory_space=pltpu.VMEM)
    attended = pl.pallas_call(
        lambda *refs: exchange_kernel(far, *refs),
        out_shape=jax.ShapeDtypeStruct((own_count, lat_width), jnp.bfloat16),
        in_specs=[pl.BlockSpec(memory_space=pl.ANY)]
        + [vmem] * 5
        + [pl.BlockSpec(memory_space=pltpu.SMEM), vmem],
        out_specs=vmem,
        scratch_shapes=room(2 * far) + room(far) + room(far - 1) + [
            pltpu.VMEM((2 * far, chip_rows, lat_width), jnp.bfloat16),
            pltpu.VMEM((2, width + 16, keys), jnp.bfloat16),
            pltpu.VMEM((2 * far, width, chip_rows), jnp.float32),
            pltpu.VMEM((2 * far, 8, chip_rows), jnp.float32),
            pltpu.VMEM((own_count, width), jnp.bfloat16),
            pltpu.VMEM((own_count, width), jnp.bfloat16),
            pltpu.VMEM((keys, 128), jnp.bfloat16),
            pltpu.VMEM((tokens, 128), jnp.bfloat16),
            pltpu.VMEM((slabs, 128), jnp.float32),
            pltpu.VMEM((slabs, 128), jnp.float32),
            pltpu.VMEM((chip_rows, slabs * head_rows), jnp.bfloat16),
            pltpu.SemaphoreType.DMA((4, 2 * far)),
            pltpu.SemaphoreType.DMA((4, far)),
            pltpu.SemaphoreType.DMA((4, far - 1)),
            pltpu.SemaphoreType.DMA((2 * far,)),
            pltpu.SemaphoreType.DMA((2,)),
        ],
        compiler_params=pltpu.CompilerParams(
            collective_id=0, has_side_effects=True, vmem_limit_bytes=60 * 1024 * 1024
        ),
        cost_estimate=pl.CostEstimate(
            flops=2 * rows * keys * (2 * lat_width + rope_width),
            bytes_accessed=2 * (rows + keys) * (lat_width + rope_width),
            transcendentals=rows * keys,
        ),
    )(
        q_latent.reshape(chips, chip_rows, lat_width),
        q_rope.reshape(chips, 2 * own_heads, tokens * rope_width),
        cache_latent, cache_rope, new_latent, new_rope, removed.T,
        jnp.asarray(rope_tables(rope_width)),
    )
    return attended.reshape(own_heads, tokens, lat_width)


def solution(mesh):
    in_specs = (
        P(None, "req", None),
        P(None, "req"),
        P(("req", "ctx"), None, None),
        P(("req", "ctx"), None, None),
        P("req", None),
        P("req", None),
        P("req", None),
    )
    out_specs = P("ctx", "req", None)
    return jax.shard_map(shards, mesh=mesh, in_specs=in_specs, out_specs=out_specs, check_vma=False)
```

```python
import jax
import jax.numpy as jnp
import numpy as np
from jax import lax
from jax.experimental import pallas as pl
from jax.experimental.pallas import tpu as pltpu
from jax.sharding import PartitionSpec as P

floor_value = -1e30
score_scale = 192.0 ** (-0.5)


def rope_tables(rope_width):
    halves = rope_width // 2
    frequencies = 10000.0 ** (-2.0 * np.arange(halves) / rope_width)
    coarse = np.mod(4096.0 * frequencies, 2.0 * np.pi)
    middle = np.mod(64.0 * frequencies, 2.0 * np.pi)
    tables = np.zeros((halves + 8, 128), np.float32)
    for digit, table in enumerate([coarse, middle, frequencies]):
        tables[:halves, digit] = table
        tables[halves + digit] = np.tile(table, 128 // halves)
    return tables


def angles_of(rows, coarse, middle, lowest):
    upper_part = (rows >> 12).astype(jnp.float32)
    centre_part = ((rows >> 6) & 63).astype(jnp.float32)
    lowest_part = (rows & 63).astype(jnp.float32)
    return upper_part * coarse + centre_part * middle + lowest_part * lowest


def span_scalars(removed_ref, first_block, local_blocks, total_blocks, block_rows):
    inside = [0] * local_blocks
    drops = [0] * local_blocks
    gone = 0
    for span in range(removed_ref.shape[1]):
        first, last = removed_ref[0, span], removed_ref[1, span]
        gone = gone + (last - first)
        for b in range(local_blocks):
            block = first_block + b
            inside[b] = inside[b] + jnp.where((block >= first) & (block < last), 1, 0)
            drops[b] = drops[b] + jnp.minimum(jnp.maximum(block, first), last) - first
    return inside, [block_rows * drop for drop in drops], block_rows * (total_blocks - gone)


def turn_slab(slab, cosine, signed_sine, rope_width):
    halves = rope_width // 2
    lane = lax.broadcasted_iota(jnp.int32, slab.shape, 1)
    swapped = jnp.where(
        lane % rope_width < halves, pltpu.roll(slab, 128 - halves, 1), pltpu.roll(slab, halves, 1)
    )
    return slab * cosine + swapped * signed_sine


code_limit = 32767.0
exponent_scale = score_scale * 1.4426950408889634
tiny_peak = 1e-30
nt_dims = (((1,), (1,)), ((), ()))
tn_dims = (((0,), (0,)), ((), ()))


def block_weights(q, qr, lat_ref, keys, inside):
    blocks, block_rows, lat_width = lat_ref.shape
    latents = lat_ref[...].reshape(blocks * block_rows, lat_width)
    scores = (
        lax.dot_general(latents, q, nt_dims, preferred_element_type=jnp.float32)
        + lax.dot_general(keys, qr, nt_dims, preferred_element_type=jnp.float32)
    )
    lifted, weights = [], []
    for b in range(blocks):
        part = scores[b * block_rows : (b + 1) * block_rows]
        block_max = jnp.max(part, axis=0, keepdims=True)
        weights.append(jnp.exp2((part - block_max) * exponent_scale).astype(jnp.bfloat16))
        lifted.append(jnp.where(inside[b] == 0, block_max * score_scale, floor_value))
    top = lifted[0]
    for b in range(1, blocks):
        top = jnp.maximum(top, lifted[b])
    factors = [jnp.where(inside[b] == 0, jnp.exp(lifted[b] - top), 0.0) for b in range(blocks)]
    return top, weights, factors


def weighted(columns, weights, factors):
    block_rows = weights[0].shape[0]
    return sum(
        jnp.dot(
            columns[:, b * block_rows : (b + 1) * block_rows],
            weights[b],
            preferred_element_type=jnp.float32,
        )
        * factors[b]
        for b in range(len(weights))
    )


def merge(one, other):
    top = jnp.maximum(one[0], other[0])
    left, right = jnp.exp(one[0] - top), jnp.exp(other[0] - top)
    return top, one[1] * left + other[1] * right, one[2] * left + other[2] * right


def put_state(state, code_ref, meta_ref, slot):
    top, total, acc = state
    peak = jnp.maximum(jnp.max(jnp.abs(acc), axis=0, keepdims=True), tiny_peak)
    code_ref[slot] = jnp.round(acc * (code_limit / peak)).astype(jnp.int32).astype(jnp.int16)
    meta_ref[slot, 0:1] = top
    meta_ref[slot, 1:2] = total
    meta_ref[slot, 2:3] = peak * (1.0 / code_limit)


def get_state(code_ref, meta_ref, slot):
    acc = code_ref[slot].astype(jnp.int32).astype(jnp.float32) * meta_ref[slot, 2:3]
    return meta_ref[slot, 0:1], meta_ref[slot, 1:2], acc


def new_state(q, qr, lat, half, keys):
    tokens, rows = lat.shape[0], q.shape[0]
    scores = (
        lax.dot_general(lat, q, nt_dims, preferred_element_type=jnp.float32)
        + lax.dot_general(keys, qr, nt_dims, preferred_element_type=jnp.float32)
    ) * score_scale
    token = lax.broadcasted_iota(jnp.int32, (tokens, rows), 1) % tokens
    causal = lax.broadcasted_iota(jnp.int32, (tokens, rows), 0) <= token
    masked = jnp.where(causal, scores, floor_value)
    top = jnp.max(masked, axis=0, keepdims=True)
    weights = jnp.where(causal, jnp.exp(masked - top), 0.0).astype(jnp.bfloat16)
    total = jnp.sum(weights.astype(jnp.float32), axis=0, keepdims=True)
    return top, total, lax.dot_general(half, weights, tn_dims, preferred_element_type=jnp.float32)


def exchange_kernel(
    far, q_ref, rope_ref, lat_ref, cache_rope_ref, new_lat_ref, new_rope_ref, removed_ref, table_ref, out_ref,
    core_out, core_in, core_out_meta, core_in_meta,
    pair_out, pair_in, pair_out_meta, pair_in_meta,
    far_out, far_in, far_out_meta, far_in_meta,
    q_buf, columns, held_acc, held_rows, swap_out, swap_in,
    key_rows, new_keys, slab_cos, slab_sin, pick,
    core_sems, pair_sems, far_sems, q_sems, swap_sems,
):
    own, lat_width = out_ref.shape
    width = lat_width // 2
    me = lax.axis_index("ctx")
    core, pair, place = me % 2, (me // 2) % 2, me // 4

    def index_of(place_id, pair_id, core_id):
        return (place_id * 2 + pair_id) * 2 + core_id

    bits = far.bit_length() - 1

    def flipped(bit):
        return (1 - place // 2**bit % 2 * 2) * 2**bit

    def place_at(step):
        apart = far - 1 - step
        return place + sum(flipped(bit) * (apart // 2**bit % 2) for bit in range(bits))

    def next_place(step):
        apart = far - 1 - step
        return place + sum(
            flipped(bit) * jnp.where(apart % 2 ** (bit + 1) == 2**bit, 1, 0) for bit in range(bits)
        )

    def chip_at(step):
        pair_id = (pair + 1 + step // far) % 2
        return place_at(step % far) * 2 + pair_id

    def q_copy(step):
        return pltpu.make_async_copy(q_ref.at[chip_at(step)], q_buf.at[step], q_sems.at[step])

    def fetch(step, nothing):
        q_copy(step).start()
        q_copy(far + step).start()
        return nothing

    lax.fori_loop(0, far, fetch, 0)
    sibling = index_of(place, pair, 1 - core)
    partner = index_of(place, 1 - pair, core)
    barrier = pltpu.get_barrier_semaphore()
    for other in [sibling, partner]:
        pl.semaphore_signal(barrier, 1, device_id={"ctx": other})

    for bit in range(bits):
        other = index_of(place + flipped(bit), pair, core)
        pl.semaphore_signal(barrier, 1, device_id={"ctx": other})
    blocks, block_rows = lat_ref.shape[:2]
    tokens, rope_width = new_rope_ref.shape
    halves, group = rope_width // 2, 128 // rope_width
    slabs = tokens // group
    turned = lat_ref[...].reshape(columns.shape[2], lat_width).T
    columns[0, :width] = turned[:width]
    columns[1, :width] = turned[width:]
    for side in range(2):
        columns[side, width:] = jnp.ones((16, columns.shape[2]), jnp.bfloat16)
    inside, drops, kept_rows = span_scalars(
        removed_ref, me * blocks, blocks, blocks * 4 * far, block_rows
    )
    along = [table_ref[halves + digit : halves + digit + 1] for digit in range(3)]
    down = [table_ref[:halves, digit : digit + 1] for digit in range(3)]

    def signed(sine):
        lane = lax.broadcasted_iota(jnp.int32, sine.shape, 1)
        return jnp.where(lane % rope_width < halves, -sine, sine)

    row = lax.broadcasted_iota(jnp.int32, (slabs, 128), 0)
    lane = lax.broadcasted_iota(jnp.int32, (slabs, 128), 1)
    angles = angles_of(kept_rows + row * group + lane // rope_width, *along)
    slab_cos[...] = jnp.cos(angles)
    slab_sin[...] = signed(jnp.sin(angles))
    angles = angles_of(kept_rows + lax.broadcasted_iota(jnp.int32, (tokens, 128), 0), *along)
    fresh_rope = jnp.concatenate([new_rope_ref[...].astype(jnp.float32)] * group, axis=1)
    new_keys[...] = turn_slab(
        fresh_rope, jnp.cos(angles), signed(jnp.sin(angles)), rope_width
    ).astype(jnp.bfloat16)
    lane = lax.broadcasted_iota(jnp.int32, (halves, 128), 1)
    dropped = jnp.zeros((halves, 128), jnp.int32)
    for b in range(blocks):
        dropped = jnp.where(lane == b, drops[b], dropped)
    angles = angles_of(dropped, *down)
    cosine, sine = jnp.cos(angles), -jnp.sin(angles)
    for b in range(blocks):
        c, s = cosine[:, b : b + 1], sine[:, b : b + 1]
        first = cache_rope_ref[b, :halves].astype(jnp.float32)
        second = cache_rope_ref[b, halves:].astype(jnp.float32)
        keys = jnp.concatenate([first * c - second * s, first * s + second * c] * group, axis=0)
        key_rows[b * block_rows : (b + 1) * block_rows] = keys.T.astype(jnp.bfloat16)
    heads = rope_ref.shape[1]
    head_rows = pick.shape[1] // slabs
    row = lax.broadcasted_iota(jnp.int32, pick.shape, 0)
    column = lax.broadcasted_iota(jnp.int32, pick.shape, 1)
    chosen = (row % tokens) // group * head_rows + row // tokens
    pick[...] = jnp.where(column == chosen, 1.0, 0.0).astype(jnp.bfloat16)

    def rope_rows(chip):
        values = rope_ref[chip].astype(jnp.float32)
        if head_rows > heads:
            spare = jnp.zeros((head_rows - heads, values.shape[1]), jnp.float32)
            values = jnp.concatenate([values, spare], axis=0)
        turned = [
            turn_slab(
                values[:, j * 128 : (j + 1) * 128],
                slab_cos[j : j + 1],
                slab_sin[j : j + 1],
                rope_width,
            )
            for j in range(slabs)
        ]
        stacked = jnp.concatenate(turned, axis=0).astype(jnp.bfloat16)
        rows = jnp.dot(pick[...], stacked, preferred_element_type=jnp.float32)
        row = lax.broadcasted_iota(jnp.int32, rows.shape, 0)
        lane = lax.broadcasted_iota(jnp.int32, rows.shape, 1)
        own_lanes = lane // rope_width == row % tokens % group
        return jnp.where(own_lanes, rows, 0.0).astype(jnp.bfloat16)

    pl.semaphore_wait(barrier, bits + 2)

    def copies(source, landing, source_meta, landing_meta, sems, slot, target):
        return [
            pltpu.make_async_remote_copy(
                src_ref=a.at[slot],
                dst_ref=b.at[slot],
                send_sem=sems.at[2 * kind, slot],
                recv_sem=sems.at[2 * kind + 1, slot],
                device_id={"ctx": target},
            )
            for kind, (a, b) in enumerate([(source, landing), (source_meta, landing_meta)])
        ]

    def core_copies(slot):
        return copies(core_out, core_in, core_out_meta, core_in_meta, core_sems, slot, sibling)

    def pair_copies(slot):
        return copies(pair_out, pair_in, pair_out_meta, pair_in_meta, pair_sems, slot, partner)

    def far_copies(slot):
        target = index_of(next_place(slot), pair, core)
        return copies(far_out, far_in, far_out_meta, far_in_meta, far_sems, slot, target)

    def start(both):
        for copy in both:
            copy.start()

    def landed(both):
        for copy in both:
            copy.wait_recv()

    def put_held(state, slot):
        held_rows[slot, 0:1] = state[0]
        held_rows[slot, 1:2] = state[1]
        held_acc[slot] = state[2]

    def get_held(slot):
        return held_rows[slot, 0:1], held_rows[slot, 1:2], held_acc[slot]

    def with_sibling(slot):
        landed(core_copies(slot))
        return merge(get_held(slot), get_state(core_in, core_in_meta, slot))

    def gather(step):
        state = with_sibling(far + step)
        landed(pair_copies(step))
        put_held(merge(state, get_state(pair_in, pair_in_meta, step)), far + step)
        for bit in range(bits):

            @pl.when((far - 1 - step) % 2 ** (bit + 1) == 0)
            def take_far():
                landed(far_copies(step - 2**bit))
                arrived = get_state(far_in, far_in_meta, step - 2**bit)
                put_held(merge(get_held(far + step), arrived), far + step)

    def to_far(step):
        gather(step)
        put_state(get_held(far + step), far_out, far_out_meta, step)
        start(far_copies(step))

    def chip_step(step):
        q_copy(step).wait()
        top, weights, factors = block_weights(
            q_buf[step], rope_rows(chip_at(step)), lat_ref, key_rows[...], inside
        )
        theirs = weighted(columns[1 - core], weights, factors)
        total = theirs[width : width + 1]
        put_state((top, total, theirs[:width]), core_out, core_out_meta, step)
        start(core_copies(step))
        put_held((top, total, weighted(columns[core, :width], weights, factors)), step)

    chip_step(0)

    def round_of(step, nothing):
        @pl.when(step < far - 1)
        def ahead():
            chip_step(step + 1)

        put_state(with_sibling(step), pair_out, pair_out_meta, step)
        start(pair_copies(step))

        @pl.when(step >= 1)
        def onward():
            to_far(step - 1)

        chip_step(far + step)
        return nothing

    lax.fori_loop(0, far, round_of, 0)
    last = 2 * far - 1
    half = jnp.where(core == 0, new_lat_ref[:, :width], new_lat_ref[:, width:])
    fresh = new_state(
        q_buf[last], rope_rows(chip_at(last)), new_lat_ref[...], half, new_keys[...]
    )
    gather(far - 1)

    top, total, acc = merge(get_held(last), fresh)
    done = acc / total
    spare = -done.shape[1] % 128
    if spare:
        done = jnp.concatenate([done, jnp.zeros((width, spare), jnp.float32)], axis=1)
    done = done.T
    first, second = done[:own], done[own : 2 * own]
    swap_out[...] = jnp.where(core == 0, second, first).astype(out_ref.dtype)
    swap = pltpu.make_async_remote_copy(
        src_ref=swap_out,
        dst_ref=swap_in,
        send_sem=swap_sems.at[0],
        recv_sem=swap_sems.at[1],
        device_id={"ctx": sibling},
    )
    swap.start()
    kept = jnp.where(core == 0, first, second)

    def sent(make, count):
        def step_of(step, nothing):
            for copy in make(step):
                copy.wait_send()
            return nothing

        lax.fori_loop(0, count, step_of, 0)

    sent(core_copies, 2 * far)
    sent(pair_copies, far)
    sent(far_copies, far - 1)
    swap.wait()
    other = swap_in[...].astype(jnp.float32)
    out_ref[:, :width] = jnp.where(core == 0, kept, other).astype(out_ref.dtype)
    out_ref[:, width:] = jnp.where(core == 0, other, kept).astype(out_ref.dtype)


def shards(q_latent, q_rope, cache_latent, cache_rope, new_latent, new_rope, removed):
    devices = lax.axis_size("ctx")
    local_blocks, block_rows, lat_width = cache_latent.shape
    head_count, tokens = (q_latent.shape[0], q_latent.shape[1])
    rope_width = new_rope.shape[1]
    own_heads = head_count // devices
    own_count = own_heads * tokens
    far = devices // 4
    chips = devices // 2
    chip_rows = 2 * own_count
    width = lat_width // 2
    rows = head_count * tokens
    keys = local_blocks * block_rows
    slabs = tokens * rope_width // 128
    head_rows = -(-2 * own_heads // 8) * 8

    def room(slots):
        return [pltpu.VMEM((slots, width, chip_rows), jnp.int16)] * 2 + [
            pltpu.VMEM((slots, 8, chip_rows), jnp.float32)
        ] * 2

    vmem = pl.BlockSpec(memory_space=pltpu.VMEM)
    attended = pl.pallas_call(
        lambda *refs: exchange_kernel(far, *refs),
        out_shape=jax.ShapeDtypeStruct((own_count, lat_width), jnp.bfloat16),
        in_specs=[pl.BlockSpec(memory_space=pl.ANY)]
        + [vmem] * 5
        + [pl.BlockSpec(memory_space=pltpu.SMEM), vmem],
        out_specs=vmem,
        scratch_shapes=room(2 * far) + room(far) + room(far - 1) + [
            pltpu.VMEM((2 * far, chip_rows, lat_width), jnp.bfloat16),
            pltpu.VMEM((2, width + 16, keys), jnp.bfloat16),
            pltpu.VMEM((2 * far, width, chip_rows), jnp.float32),
            pltpu.VMEM((2 * far, 8, chip_rows), jnp.float32),
            pltpu.VMEM((own_count, width), jnp.bfloat16),
            pltpu.VMEM((own_count, width), jnp.bfloat16),
            pltpu.VMEM((keys, 128), jnp.bfloat16),
            pltpu.VMEM((tokens, 128), jnp.bfloat16),
            pltpu.VMEM((slabs, 128), jnp.float32),
            pltpu.VMEM((slabs, 128), jnp.float32),
            pltpu.VMEM((chip_rows, slabs * head_rows), jnp.bfloat16),
            pltpu.SemaphoreType.DMA((4, 2 * far)),
            pltpu.SemaphoreType.DMA((4, far)),
            pltpu.SemaphoreType.DMA((4, far - 1)),
            pltpu.SemaphoreType.DMA((2 * far,)),
            pltpu.SemaphoreType.DMA((2,)),
        ],
        compiler_params=pltpu.CompilerParams(
            collective_id=0, has_side_effects=True, vmem_limit_bytes=53 * 1024 * 1024
        ),
        cost_estimate=pl.CostEstimate(
            flops=2 * rows * keys * (2 * lat_width + rope_width),
            bytes_accessed=2 * (rows + keys) * (lat_width + rope_width),
            transcendentals=rows * keys,
        ),
    )(
        q_latent.reshape(chips, chip_rows, lat_width),
        q_rope.reshape(chips, 2 * own_heads, tokens * rope_width),
        cache_latent, cache_rope, new_latent, new_rope, removed.T,
        jnp.asarray(rope_tables(rope_width)),
    )
    return attended.reshape(own_heads, tokens, lat_width)


def solution(mesh):
    in_specs = (
        P(None, "req", None),
        P(None, "req"),
        P(("req", "ctx"), None, None),
        P(("req", "ctx"), None, None),
        P("req", None),
        P("req", None),
        P("req", None),
    )
    out_specs = P("ctx", "req", None)
    return jax.shard_map(shards, mesh=mesh, in_specs=in_specs, out_specs=out_specs, check_vma=False)
```

```python
import jax
import jax.numpy as jnp
import numpy as np
from jax import lax
from jax.experimental import pallas as pl
from jax.experimental.pallas import tpu as pltpu
from jax.sharding import PartitionSpec as P

floor_value = -1e30
score_scale = 192.0 ** (-0.5)


def rope_tables(rope_width):
    halves = rope_width // 2
    frequencies = 10000.0 ** (-2.0 * np.arange(halves) / rope_width)
    coarse = np.mod(4096.0 * frequencies, 2.0 * np.pi)
    middle = np.mod(64.0 * frequencies, 2.0 * np.pi)
    tables = np.zeros((halves + 8, 128), np.float32)
    for digit, table in enumerate([coarse, middle, frequencies]):
        tables[:halves, digit] = table
        tables[halves + digit] = np.tile(table, 128 // halves)
    return tables


def angles_of(rows, coarse, middle, lowest):
    upper_part = (rows >> 12).astype(jnp.float32)
    centre_part = ((rows >> 6) & 63).astype(jnp.float32)
    lowest_part = (rows & 63).astype(jnp.float32)
    return upper_part * coarse + centre_part * middle + lowest_part * lowest


def span_scalars(removed_ref, first_block, local_blocks, total_blocks, block_rows):
    inside = [0] * local_blocks
    drops = [0] * local_blocks
    gone = 0
    for span in range(removed_ref.shape[1]):
        first, last = removed_ref[0, span], removed_ref[1, span]
        gone = gone + (last - first)
        for b in range(local_blocks):
            block = first_block + b
            inside[b] = inside[b] + jnp.where((block >= first) & (block < last), 1, 0)
            drops[b] = drops[b] + jnp.minimum(jnp.maximum(block, first), last) - first
    return inside, [block_rows * drop for drop in drops], block_rows * (total_blocks - gone)


def turn_slab(slab, cosine, signed_sine, rope_width):
    halves = rope_width // 2
    lane = lax.broadcasted_iota(jnp.int32, slab.shape, 1)
    swapped = jnp.where(
        lane % rope_width < halves, pltpu.roll(slab, 128 - halves, 1), pltpu.roll(slab, halves, 1)
    )
    return slab * cosine + swapped * signed_sine


code_limit = 32767.0
exponent_scale = score_scale * 1.4426950408889634
tiny_peak = 1e-30
nt_dims = (((1,), (1,)), ((), ()))
tn_dims = (((0,), (0,)), ((), ()))


def block_weights(q, qr, lat_ref, keys, inside):
    blocks, block_rows, lat_width = lat_ref.shape
    latents = lat_ref[...].reshape(blocks * block_rows, lat_width)
    scores = (
        lax.dot_general(latents, q, nt_dims, preferred_element_type=jnp.float32)
        + lax.dot_general(keys, qr, nt_dims, preferred_element_type=jnp.float32)
    )
    lifted, weights = [], []
    for b in range(blocks):
        part = scores[b * block_rows : (b + 1) * block_rows]
        block_max = jnp.max(part, axis=0, keepdims=True)
        weights.append(jnp.exp2((part - block_max) * exponent_scale).astype(jnp.bfloat16))
        lifted.append(jnp.where(inside[b] == 0, block_max * score_scale, floor_value))
    top = lifted[0]
    for b in range(1, blocks):
        top = jnp.maximum(top, lifted[b])
    factors = [jnp.where(inside[b] == 0, jnp.exp(lifted[b] - top), 0.0) for b in range(blocks)]
    return top, weights, factors


def weighted(columns, weights, factors):
    block_rows = weights[0].shape[0]
    return sum(
        jnp.dot(
            columns[:, b * block_rows : (b + 1) * block_rows],
            weights[b],
            preferred_element_type=jnp.float32,
        )
        * factors[b]
        for b in range(len(weights))
    )


def merge(one, other):
    top = jnp.maximum(one[0], other[0])
    left, right = jnp.exp(one[0] - top), jnp.exp(other[0] - top)
    return top, one[1] * left + other[1] * right, one[2] * left + other[2] * right


def put_state(state, code_ref, meta_ref, slot):
    top, total, acc = state
    peak = jnp.maximum(jnp.max(jnp.abs(acc), axis=0, keepdims=True), tiny_peak)
    code_ref[slot] = jnp.round(acc * (code_limit / peak)).astype(jnp.int32).astype(jnp.int16)
    meta_ref[slot, 0:1] = top
    meta_ref[slot, 1:2] = total
    meta_ref[slot, 2:3] = peak * (1.0 / code_limit)


def get_state(code_ref, meta_ref, slot):
    acc = code_ref[slot].astype(jnp.int32).astype(jnp.float32) * meta_ref[slot, 2:3]
    return meta_ref[slot, 0:1], meta_ref[slot, 1:2], acc


def new_state(q, qr, lat, half, keys):
    tokens, rows = lat.shape[0], q.shape[0]
    scores = (
        lax.dot_general(lat, q, nt_dims, preferred_element_type=jnp.float32)
        + lax.dot_general(keys, qr, nt_dims, preferred_element_type=jnp.float32)
    ) * score_scale
    token = lax.broadcasted_iota(jnp.int32, (tokens, rows), 1) % tokens
    causal = lax.broadcasted_iota(jnp.int32, (tokens, rows), 0) <= token
    masked = jnp.where(causal, scores, floor_value)
    top = jnp.max(masked, axis=0, keepdims=True)
    weights = jnp.where(causal, jnp.exp(masked - top), 0.0).astype(jnp.bfloat16)
    total = jnp.sum(weights.astype(jnp.float32), axis=0, keepdims=True)
    return top, total, lax.dot_general(half, weights, tn_dims, preferred_element_type=jnp.float32)


def exchange_kernel(
    far, q_ref, rope_ref, lat_ref, cache_rope_ref, new_lat_ref, new_rope_ref, removed_ref, table_ref, out_ref,
    core_out, core_in, core_out_meta, core_in_meta,
    pair_out, pair_in, pair_out_meta, pair_in_meta,
    far_out, far_in, far_out_meta, far_in_meta,
    q_buf, columns, held_acc, held_rows, swap_out, swap_in,
    key_rows, slab_cos, slab_sin, pick,
    core_sems, pair_sems, far_sems, q_sems, swap_sems,
):
    own, lat_width = out_ref.shape
    width = lat_width // 2
    me = lax.axis_index("ctx")
    core, pair, place = me % 2, (me // 2) % 2, me // 4

    def index_of(place_id, pair_id, core_id):
        return (place_id * 2 + pair_id) * 2 + core_id

    bits = far.bit_length() - 1

    def flipped(bit):
        return (1 - place // 2**bit % 2 * 2) * 2**bit

    def place_at(step):
        apart = far - 1 - step
        return place + sum(flipped(bit) * (apart // 2**bit % 2) for bit in range(bits))

    def next_place(step):
        apart = far - 1 - step
        return place + sum(
            flipped(bit) * jnp.where(apart % 2 ** (bit + 1) == 2**bit, 1, 0) for bit in range(bits)
        )

    def chip_at(step):
        pair_id = (pair + 1 + step // far) % 2
        return place_at(step % far) * 2 + pair_id

    def q_copy(step):
        return pltpu.make_async_copy(q_ref.at[chip_at(step)], q_buf.at[step], q_sems.at[step])

    def fetch(step, nothing):
        q_copy(step).start()
        q_copy(far + step).start()
        return nothing

    lax.fori_loop(0, far, fetch, 0)
    sibling = index_of(place, pair, 1 - core)
    partner = index_of(place, 1 - pair, core)
    barrier = pltpu.get_barrier_semaphore()
    for other in [sibling, partner]:
        pl.semaphore_signal(barrier, 1, device_id={"ctx": other})

    for bit in range(bits):
        other = index_of(place + flipped(bit), pair, core)
        pl.semaphore_signal(barrier, 1, device_id={"ctx": other})
    blocks, block_rows = lat_ref.shape[:2]
    tokens, rope_width = new_rope_ref.shape
    halves, group = rope_width // 2, 128 // rope_width
    slabs = tokens // group
    turned = lat_ref[...].reshape(columns.shape[2], lat_width).T
    columns[0, :width] = turned[:width]
    columns[1, :width] = turned[width:]
    for side in range(2):
        columns[side, width:] = jnp.ones((16, columns.shape[2]), jnp.bfloat16)
    inside, drops, kept_rows = span_scalars(
        removed_ref, me * blocks, blocks, blocks * 4 * far, block_rows
    )
    along = [table_ref[halves + digit : halves + digit + 1] for digit in range(3)]
    down = [table_ref[:halves, digit : digit + 1] for digit in range(3)]

    def signed(sine):
        lane = lax.broadcasted_iota(jnp.int32, sine.shape, 1)
        return jnp.where(lane % rope_width < halves, -sine, sine)

    row = lax.broadcasted_iota(jnp.int32, (slabs, 128), 0)
    lane = lax.broadcasted_iota(jnp.int32, (slabs, 128), 1)
    angles = angles_of(kept_rows + row * group + lane // rope_width, *along)
    slab_cos[...] = jnp.cos(angles)
    slab_sin[...] = signed(jnp.sin(angles))
    lane = lax.broadcasted_iota(jnp.int32, (halves, 128), 1)
    dropped = jnp.zeros((halves, 128), jnp.int32)
    for b in range(blocks):
        dropped = jnp.where(lane == b, drops[b], dropped)
    angles = angles_of(dropped, *down)
    cosine, sine = jnp.cos(angles), -jnp.sin(angles)
    for b in range(blocks):
        c, s = cosine[:, b : b + 1], sine[:, b : b + 1]
        first = cache_rope_ref[b, :halves].astype(jnp.float32)
        second = cache_rope_ref[b, halves:].astype(jnp.float32)
        keys = jnp.concatenate([first * c - second * s, first * s + second * c] * group, axis=0)
        key_rows[b * block_rows : (b + 1) * block_rows] = keys.T.astype(jnp.bfloat16)
    heads = rope_ref.shape[1]
    head_rows = pick.shape[1] // slabs
    row = lax.broadcasted_iota(jnp.int32, pick.shape, 0)
    column = lax.broadcasted_iota(jnp.int32, pick.shape, 1)
    chosen = (row % tokens) // group * head_rows + row // tokens
    pick[...] = jnp.where(column == chosen, 1.0, 0.0).astype(jnp.bfloat16)

    def rope_rows(chip):
        values = rope_ref[chip].astype(jnp.float32)
        if head_rows > heads:
            spare = jnp.zeros((head_rows - heads, values.shape[1]), jnp.float32)
            values = jnp.concatenate([values, spare], axis=0)
        turned = [
            turn_slab(
                values[:, j * 128 : (j + 1) * 128],
                slab_cos[j : j + 1],
                slab_sin[j : j + 1],
                rope_width,
            )
            for j in range(slabs)
        ]
        stacked = jnp.concatenate(turned, axis=0).astype(jnp.bfloat16)
        rows = jnp.dot(pick[...], stacked, preferred_element_type=jnp.float32)
        row = lax.broadcasted_iota(jnp.int32, rows.shape, 0)
        lane = lax.broadcasted_iota(jnp.int32, rows.shape, 1)
        own_lanes = lane // rope_width == row % tokens % group
        return jnp.where(own_lanes, rows, 0.0).astype(jnp.bfloat16)

    pl.semaphore_wait(barrier, bits + 2)

    def copies(source, landing, source_meta, landing_meta, sems, slot, target):
        return [
            pltpu.make_async_remote_copy(
                src_ref=a.at[slot],
                dst_ref=b.at[slot],
                send_sem=sems.at[2 * kind, slot],
                recv_sem=sems.at[2 * kind + 1, slot],
                device_id={"ctx": target},
            )
            for kind, (a, b) in enumerate([(source, landing), (source_meta, landing_meta)])
        ]

    def core_copies(slot):
        return copies(core_out, core_in, core_out_meta, core_in_meta, core_sems, slot, sibling)

    def pair_copies(slot):
        return copies(pair_out, pair_in, pair_out_meta, pair_in_meta, pair_sems, slot, partner)

    def far_copies(slot):
        target = index_of(next_place(slot), pair, core)
        return copies(far_out, far_in, far_out_meta, far_in_meta, far_sems, slot, target)

    def start(both):
        for copy in both:
            copy.start()

    def landed(both):
        for copy in both:
            copy.wait_recv()

    def put_held(state, slot):
        held_rows[slot, 0:1] = state[0]
        held_rows[slot, 1:2] = state[1]
        held_acc[slot] = state[2]

    def get_held(slot):
        return held_rows[slot, 0:1], held_rows[slot, 1:2], held_acc[slot]

    def with_sibling(slot):
        landed(core_copies(slot))
        return merge(get_held(slot), get_state(core_in, core_in_meta, slot))

    def gather(step):
        state = with_sibling(far + step)
        landed(pair_copies(step))
        put_held(merge(state, get_state(pair_in, pair_in_meta, step)), far + step)
        for bit in range(bits):

            @pl.when((far - 1 - step) % 2 ** (bit + 1) == 0)
            def take_far():
                landed(far_copies(step - 2**bit))
                arrived = get_state(far_in, far_in_meta, step - 2**bit)
                put_held(merge(get_held(far + step), arrived), far + step)

    def to_far(step):
        gather(step)
        put_state(get_held(far + step), far_out, far_out_meta, step)
        start(far_copies(step))

    def chip_step(step):
        q_copy(step).wait()
        top, weights, factors = block_weights(
            q_buf[step], rope_rows(chip_at(step)), lat_ref, key_rows[...], inside
        )
        theirs = weighted(columns[1 - core], weights, factors)
        total = theirs[width : width + 1]
        put_state((top, total, theirs[:width]), core_out, core_out_meta, step)
        start(core_copies(step))
        put_held((top, total, weighted(columns[core, :width], weights, factors)), step)

    chip_step(0)

    def round_of(step, nothing):
        @pl.when(step < far - 1)
        def ahead():
            chip_step(step + 1)

        put_state(with_sibling(step), pair_out, pair_out_meta, step)
        start(pair_copies(step))

        @pl.when(step >= 1)
        def onward():
            to_far(step - 1)

        chip_step(far + step)
        return nothing

    lax.fori_loop(0, far, round_of, 0)
    last = 2 * far - 1
    half = jnp.where(core == 0, new_lat_ref[:, :width], new_lat_ref[:, width:])
    angles = angles_of(kept_rows + lax.broadcasted_iota(jnp.int32, (tokens, 128), 0), *along)
    fresh_rope = jnp.concatenate([new_rope_ref[...].astype(jnp.float32)] * group, axis=1)
    fresh_keys = turn_slab(
        fresh_rope, jnp.cos(angles), signed(jnp.sin(angles)), rope_width
    ).astype(jnp.bfloat16)
    fresh = new_state(
        q_buf[last], rope_rows(chip_at(last)), new_lat_ref[...], half, fresh_keys
    )
    gather(far - 1)

    top, total, acc = merge(get_held(last), fresh)
    done = acc / total
    spare = -done.shape[1] % 128
    if spare:
        done = jnp.concatenate([done, jnp.zeros((width, spare), jnp.float32)], axis=1)
    done = done.T
    first, second = done[:own], done[own : 2 * own]
    swap_out[...] = jnp.where(core == 0, second, first).astype(out_ref.dtype)
    swap = pltpu.make_async_remote_copy(
        src_ref=swap_out,
        dst_ref=swap_in,
        send_sem=swap_sems.at[0],
        recv_sem=swap_sems.at[1],
        device_id={"ctx": sibling},
    )
    swap.start()
    kept = jnp.where(core == 0, first, second)

    def sent(make, count):
        def step_of(step, nothing):
            for copy in make(step):
                copy.wait_send()
            return nothing

        lax.fori_loop(0, count, step_of, 0)

    sent(core_copies, 2 * far)
    sent(pair_copies, far)
    sent(far_copies, far - 1)
    swap.wait()
    other = swap_in[...].astype(jnp.float32)
    out_ref[:, :width] = jnp.where(core == 0, kept, other).astype(out_ref.dtype)
    out_ref[:, width:] = jnp.where(core == 0, other, kept).astype(out_ref.dtype)


def shards(q_latent, q_rope, cache_latent, cache_rope, new_latent, new_rope, removed):
    devices = lax.axis_size("ctx")
    local_blocks, block_rows, lat_width = cache_latent.shape
    head_count, tokens = (q_latent.shape[0], q_latent.shape[1])
    rope_width = new_rope.shape[1]
    own_heads = head_count // devices
    own_count = own_heads * tokens
    far = devices // 4
    chips = devices // 2
    chip_rows = 2 * own_count
    width = lat_width // 2
    rows = head_count * tokens
    keys = local_blocks * block_rows
    slabs = tokens * rope_width // 128
    head_rows = -(-2 * own_heads // 8) * 8

    def room(slots):
        return [pltpu.VMEM((slots, width, chip_rows), jnp.int16)] * 2 + [
            pltpu.VMEM((slots, 8, chip_rows), jnp.float32)
        ] * 2

    vmem = pl.BlockSpec(memory_space=pltpu.VMEM)
    attended = pl.pallas_call(
        lambda *refs: exchange_kernel(far, *refs),
        out_shape=jax.ShapeDtypeStruct((own_count, lat_width), jnp.bfloat16),
        in_specs=[pl.BlockSpec(memory_space=pl.ANY)]
        + [vmem] * 5
        + [pl.BlockSpec(memory_space=pltpu.SMEM), vmem],
        out_specs=vmem,
        scratch_shapes=room(2 * far) + room(far) + room(far - 1) + [
            pltpu.VMEM((2 * far, chip_rows, lat_width), jnp.bfloat16),
            pltpu.VMEM((2, width + 16, keys), jnp.bfloat16),
            pltpu.VMEM((2 * far, width, chip_rows), jnp.float32),
            pltpu.VMEM((2 * far, 8, chip_rows), jnp.float32),
            pltpu.VMEM((own_count, width), jnp.bfloat16),
            pltpu.VMEM((own_count, width), jnp.bfloat16),
            pltpu.VMEM((keys, 128), jnp.bfloat16),
            pltpu.VMEM((slabs, 128), jnp.float32),
            pltpu.VMEM((slabs, 128), jnp.float32),
            pltpu.VMEM((chip_rows, slabs * head_rows), jnp.bfloat16),
            pltpu.SemaphoreType.DMA((4, 2 * far)),
            pltpu.SemaphoreType.DMA((4, far)),
            pltpu.SemaphoreType.DMA((4, far - 1)),
            pltpu.SemaphoreType.DMA((2 * far,)),
            pltpu.SemaphoreType.DMA((2,)),
        ],
        compiler_params=pltpu.CompilerParams(
            collective_id=0, has_side_effects=True, vmem_limit_bytes=60 * 1024 * 1024
        ),
        cost_estimate=pl.CostEstimate(
            flops=2 * rows * keys * (2 * lat_width + rope_width),
            bytes_accessed=2 * (rows + keys) * (lat_width + rope_width),
            transcendentals=rows * keys,
        ),
    )(
        q_latent.reshape(chips, chip_rows, lat_width),
        q_rope.reshape(chips, 2 * own_heads, tokens * rope_width),
        cache_latent, cache_rope, new_latent, new_rope, removed.T,
        jnp.asarray(rope_tables(rope_width)),
    )
    return attended.reshape(own_heads, tokens, lat_width)


def solution(mesh):
    in_specs = (
        P(None, "req", None),
        P(None, "req"),
        P(("req", "ctx"), None, None),
        P(("req", "ctx"), None, None),
        P("req", None),
        P("req", None),
        P("req", None),
    )
    out_specs = P("ctx", "req", None)
    return jax.shard_map(shards, mesh=mesh, in_specs=in_specs, out_specs=out_specs, check_vma=False)
```
